32 devices in a mesh: ctx: 16 (over z, y, core), head: 2 (over x).
Axes of the slice: x: 2, y: 2, z: 4, core: 2. Of those that a mesh axis runs over, the one named last changes fastest.
Arguments:
- queries: bfloat16 [2048, 5120], P('ctx', 'head'), may hold values from -80 to 80
- keys: bfloat16 [2048, 1024], P('ctx', 'head'), may hold values from -4 to 4
- values: bfloat16 [2048, 1024], P('ctx', 'head'), may hold values from -6 to 6
- out_grad: bfloat16 [2048, 5120], P('ctx', 'head'), may hold values from -6 to 6
- out_weight: bfloat16 [5120, 5120], P('head'), may hold values from -0.078125 to 0.078125
- seq_lengths: int32 [4], replicated, may hold values from 1 to 1024, as said below
- prompt_lengths: int32 [4], replicated, may hold values from 1 to 127
Outputs:
- query_grad: bfloat16 [2048, 5120], P('ctx', 'head')
- key_grad: bfloat16 [2048, 1024], P('ctx', 'head')
- value_grad: bfloat16 [2048, 1024], P('ctx', 'head')
The draws below stay inside these ranges and needn't reach their ends.
Inputs may be any that keep to these rules, and one draw needn't show every extreme that they name: `seq_lengths`: the lengths sum to 2048; the first is exactly 1024.
All inputs are finite; a program needn't handle non-finite values.
Results may differ from the reference program's by a relative error of at most 0.015.
Values may be sent and summed in bfloat16 or wider, within the bound.
A program may use at most 64 MiB of HBM per device.

```python
import math
import jax
import jax.numpy as jnp
from jax import lax

D = 5120
HEADS_Q = 40
HEADS_KV = 8
HEAD_DIM = 128
TOK_DEV = 128
SEQS = 4
TOKENS = 2048


def shared_keys(key):
    drawn_keys = jax.random.truncated_normal(jax.random.fold_in(key, 11), -4.0, 4.0, (TOKENS, HEADS_KV * HEAD_DIM), jnp.float32)
    distance = 3 * TOKENS // 8
    places = jnp.arange(TOKENS, dtype=jnp.int32)
    copied = (places % 97 == 5) & (places >= distance) & (places < TOKENS // 2)
    blended = drawn_keys
    return jnp.where(copied[:, None], blended, drawn_keys)


def draw_keys(key, part):
    drawn_keys = shared_keys(key)
    return drawn_keys.astype(jnp.bfloat16)


def draw_queries(key, part):
    key = jax.random.fold_in(key, 5)
    fresh_rows = jax.random.truncated_normal(key, -4.0, 4.0, (TOKENS, HEADS_Q * HEAD_DIM), jnp.float32)
    return fresh_rows.astype(jnp.bfloat16)


def draw_seq_lengths(key, part):
    key = jax.random.fold_in(key, 7)
    half = TOKENS // 2
    inner = jnp.arange(1, half, dtype=jnp.int32)
    cuts = jnp.sort(jax.random.permutation(key, inner)[:SEQS - 2])
    edges = jnp.concatenate([jnp.zeros((1,), jnp.int32), cuts.astype(jnp.int32), jnp.full((1,), half, jnp.int32)])
    rest = (edges[1:] - edges[:-1]).astype(jnp.int32)
    return jnp.concatenate([jnp.full((1,), half, jnp.int32), rest])


def with_ends(result, stream_key, least, top_value):
    extent = result.shape
    place = [jax.random.randint(jax.random.fold_in(stream_key, axis), (), 0, extent[axis]) for axis in range(len(extent))]
    result = result.at[tuple(place)].set(least)
    longest = extent.index(max(extent))
    place[longest] = (place[longest] + 1) % extent[longest]
    return result.at[tuple(place)].set(top_value)


def shard_levels(own_key, extent, pieces, least, high):
    gain = 1.0
    for axis_at, blocks in pieces:
        heights = jax.random.uniform(jax.random.fold_in(jax.random.fold_in(own_key, 6), axis_at), (blocks,), jnp.float32, least / len(pieces), high / len(pieces))
        gain = gain * jnp.repeat(jnp.exp(heights), extent[axis_at] // blocks).reshape((-1,) + (1,) * (len(extent) - 1 - axis_at))
    return gain


def noise(stream_key, shape, deviation, most, pieces=(), kind=jnp.bfloat16):
    values = jax.random.normal(stream_key, shape, jnp.float32) * deviation
    if len(pieces) > 0:
        values = shard_levels(stream_key, shape, pieces, -0.22, 0.18) * values
    return jnp.clip(values, min=-most, max=most).astype(kind)


def setup_inputs(seed: int = 0) -> dict:
    key_of = jax.random.split(jax.random.key(seed), 8)
    queries = draw_queries(jax.random.fold_in(key_of[7], 71), 0)
    keys = draw_keys(jax.random.fold_in(key_of[7], 71), 0)
    values = noise(key_of[2], (TOKENS, HEADS_KV * HEAD_DIM), 1.0, 6.0, ((0, 16), (1, 2)))
    out_grad = noise(key_of[3], (TOKENS, D), 1.0, 6.0, ((0, 16), (1, 2)))
    out_weight = noise(key_of[4], (HEADS_Q * HEAD_DIM, D), D ** -0.5, 0.078125, ((0, 2),))
    seq_lengths = draw_seq_lengths(jax.random.fold_in(key_of[7], 71), 0)
    prompt_lengths = with_ends(jax.random.randint(key_of[6], (SEQS,), 1, TOK_DEV), jax.random.fold_in(key_of[6], 1), 1, TOK_DEV - 1).astype(jnp.int32)
    return dict(queries=queries, keys=keys, values=values, out_grad=out_grad, out_weight=out_weight, seq_lengths=seq_lengths, prompt_lengths=prompt_lengths)


NEG_LARGE = -1e+30

def segment_of(positions, bounds):
    return lax.optimization_barrier(jnp.sum((positions[:, None] >= bounds[None, :]).astype(jnp.int32), axis=1))

def layout(seq_lengths, prompt_lengths, positions):
    bounds = jnp.cumsum(seq_lengths).astype(jnp.int32)
    answer_start = bounds - seq_lengths + jnp.minimum(prompt_lengths, seq_lengths - 1)
    segment = segment_of(positions, bounds)
    labels = jnp.arange(bounds.shape[0], dtype=jnp.int32)
    picked = lax.optimization_barrier(jnp.sum(jnp.where(segment[:, None] == labels[None, :], answer_start[None, :], 0), axis=1))
    return (segment, positions >= picked)

def reference(queries, keys, values, out_grad, out_weight, seq_lengths, prompt_lengths):
    total = queries.shape[0]
    group = HEADS_Q // HEADS_KV
    scale = 1.0 / math.sqrt(HEAD_DIM)
    positions = jnp.arange(total, dtype=jnp.int32)
    segment, answer = layout(seq_lengths, prompt_lengths, positions)
    allowed = (positions[None, :] <= positions[:, None]) & (segment[None, :] == segment[:, None])
    summed = lax.dot_general(out_grad, out_weight, (((1,), (1,)), ((), ())), preferred_element_type=jnp.float32)
    grads = (summed * answer[:, None].astype(jnp.float32)).astype(jnp.bfloat16)
    query_heads = queries.reshape(total, HEADS_Q, HEAD_DIM).transpose(1, 0, 2)
    grad_heads = grads.reshape(total, HEADS_Q, HEAD_DIM).transpose(1, 0, 2)
    key_heads = jnp.repeat(keys.reshape(total, HEADS_KV, HEAD_DIM), group, axis=1).transpose(1, 0, 2)
    value_heads = jnp.repeat(values.reshape(total, HEADS_KV, HEAD_DIM), group, axis=1).transpose(1, 0, 2)

    def per_head(items):
        query, key_rows, value_rows, grad_rows = items
        scores = jnp.dot(query, key_rows.T, preferred_element_type=jnp.float32) * scale
        peak = lax.optimization_barrier(jnp.max(jnp.where(allowed, scores, NEG_LARGE), axis=1))
        mass = lax.optimization_barrier(jnp.sum(jnp.where(allowed, jnp.exp(scores - peak[:, None]), 0.0), axis=1))
        logsum = peak + jnp.log(mass)
        probs = jnp.where(allowed, jnp.exp(scores - logsum[:, None]), 0.0)
        dprobs = jnp.dot(grad_rows, value_rows.T, preferred_element_type=jnp.float32)
        delta = lax.optimization_barrier(jnp.sum(probs * dprobs, axis=1))
        dscores = (probs * (dprobs - delta[:, None])).astype(jnp.bfloat16)
        probs_half = probs.astype(jnp.bfloat16)
        dims = (((0,), (0,)), ((), ()))
        dvalue = lax.dot_general(probs_half, grad_rows, dims, preferred_element_type=jnp.float32)
        dkey = lax.dot_general(dscores, query, dims, preferred_element_type=jnp.float32) * scale
        dquery = jnp.dot(dscores, key_rows, preferred_element_type=jnp.float32) * scale
        return (dquery.astype(jnp.bfloat16), dkey, dvalue)
    dquery, dkey, dvalue = lax.map(per_head, (query_heads, key_heads, value_heads, grad_heads))
    query_grad = dquery.transpose(1, 0, 2).reshape(total, HEADS_Q * HEAD_DIM)
    key_grad = lax.optimization_barrier(jnp.sum(dkey.reshape(HEADS_KV, group, total, HEAD_DIM), axis=1))
    value_grad = lax.optimization_barrier(jnp.sum(dvalue.reshape(HEADS_KV, group, total, HEAD_DIM), axis=1))
    key_grad = key_grad.transpose(1, 0, 2).reshape(total, HEADS_KV * HEAD_DIM).astype(jnp.bfloat16)
    value_grad = value_grad.transpose(1, 0, 2).reshape(total, HEADS_KV * HEAD_DIM).astype(jnp.bfloat16)
    return (query_grad, key_grad, value_grad)
```

```python
import functools
import math

import jax
import jax.numpy as jnp
from jax import lax
from jax.experimental import pallas as pl
from jax.experimental.pallas import tpu as pltpu
from jax.sharding import PartitionSpec as P

HEADS_Q = 40
HEADS_KV = 8
HEAD_DIM = 128
GROUP = HEADS_Q // HEADS_KV
SCALE = 1.0 / math.sqrt(HEAD_DIM)
NEG_LARGE = -1e30
NT = (((1,), (1,)), ((), ()))
NN = (((1,), (0,)), ((), ()))
TN = (((0,), (0,)), ((), ()))


def dot(a, b, dims):
    return lax.dot_general(a, b, dims, preferred_element_type=jnp.float32)


def segment_facts(seq_ref, prompt_ref, positions):
    start = jnp.zeros_like(positions)
    first = jnp.zeros_like(positions)
    begin = 0
    for s in range(seq_ref.shape[0]):
        length = seq_ref[s]
        reached = positions >= begin
        start = jnp.where(reached, begin, start)
        first = jnp.where(reached, begin + jnp.minimum(prompt_ref[s], length - 1), first)
        begin = begin + length
    return start, first


def kernel(
    nctx, nhead, chunk,
    q_ref, k_ref, v_ref, og_ref, w_ref, seq_ref, prompt_ref,
    dq_ref, dk_ref, dv_ref,
    wbuf, ogbuf, acc, qs, gs, kbuf, vbuf, probs, dprobs, peak, dqt, part, sib, total, sums, ret,
    w_sem, og_send, og_recv, k_send, v_send, k_recv, v_recv, k_fwd, v_fwd,
    sib_send, sib_recv, ret_send, ret_recv,
):
    count = q_ref.shape[0]
    kv_local = k_ref.shape[1] // HEAD_DIM
    chips = nctx // 4
    features = w_ref.shape[0]
    part_width = og_ref.shape[1]
    chunks = part_width // chunk
    me = lax.axis_index("ctx")
    head = lax.axis_index("head")
    half = me // (nctx // 2)
    base = half * (nctx // 2)
    core = me % 2
    other = 1 - core
    chip = (me - base) // 2
    sibling = me + 1 - 2 * core

    def remote(src, dst, send, recv, ctx, head_at):
        return pltpu.make_async_remote_copy(
            src_ref=src, dst_ref=dst, send_sem=send, recv_sem=recv,
            device_id=(ctx, head_at), device_id_type=pl.DeviceIdType.MESH,
        )

    def same_core(p):
        return base + 2 * p + core

    def w_copy(t):
        column = ((head + t // chunks) % nhead) * part_width + (t % chunks) * chunk
        return pltpu.make_async_copy(
            w_ref.at[:, pl.ds(pl.multiple_of(column, 128), chunk)], wbuf.at[t], w_sem.at[t]
        )

    for t in range(nhead * chunks):
        w_copy(t).start()

    barrier = pltpu.get_barrier_semaphore()

    def greet(ctx, head_at):
        pl.semaphore_signal(
            barrier, inc=1, device_id=(ctx, head_at), device_id_type=pl.DeviceIdType.MESH
        )

    for o in range(1, nhead):
        greet(me, (head + o) % nhead)
    greet(sibling, head)
    for o in range(1, chips):
        greet(same_core((chip + o) % chips), head)
    pl.semaphore_wait(barrier, nhead - 1 + 1 + chips - 1)

    def og_copy(o, ch):
        return remote(
            og_ref.at[:, pl.ds(ch * chunk, chunk)], ogbuf.at[o - 1, ch],
            og_send.at[o - 1, ch], og_recv.at[o - 1, ch], me, (head + nhead - o) % nhead,
        )

    for ch in range(chunks):
        for o in range(1, nhead):
            og_copy(o, ch).start()

    def direct(ref, buf, send, recv, p):
        return remote(ref, buf.at[chip, core], send.at[p], recv.at[chip, core], same_core(p), head)

    def to_sibling(ref, buf, send, recv, p):
        return remote(ref, buf.at[p, core], send.at[p], recv.at[p, core], sibling, head)

    def arrived(ref, buf, recv, p, c):
        pltpu.make_async_copy(ref, buf.at[p, c], recv.at[p, c]).wait()

    pairs = ((k_ref, kbuf, k_send, k_recv, k_fwd), (v_ref, vbuf, v_send, v_recv, v_fwd))
    for ref, buf, send, recv, fwd in pairs:
        to_sibling(ref, buf, fwd, recv, chip).start()

        def send_direct(p, carry, ref=ref, buf=buf, send=send, recv=recv):
            direct(ref, buf, send, recv, p).start()
            return carry

        lax.fori_loop(chip + 1, chips, send_direct, 0)
        buf[chip, core] = ref[...]

    for c in range(kv_local):
        for g in range(GROUP):
            h = c * GROUP + g
            qs[c, g * count:(g + 1) * count, :] = q_ref[:, h * HEAD_DIM:(h + 1) * HEAD_DIM]

    tile = 640 if features % 640 == 0 else HEAD_DIM

    def project(rows, t, first):
        for n in range(0, features, tile):
            here = dot(rows, wbuf[t, n:n + tile, :], NT)
            if first:
                acc[:, n:n + tile] = here
            else:
                acc[:, n:n + tile] = acc[:, n:n + tile] + here

    w_copy(0).wait()
    project(og_ref[:, :chunk], 0, True)

    def own_step(t, carry):
        w_copy(t).wait()
        project(og_ref[:, pl.ds(pl.multiple_of(t * chunk, chunk), chunk)], t, False)
        return carry

    lax.fori_loop(1, chunks, own_step, 0)

    key_rows = 2 * count
    columns = GROUP * count
    query_pos = me * count + lax.broadcasted_iota(jnp.int32, (1, count), 1)
    query_start, _ = segment_facts(seq_ref, prompt_ref, query_pos)
    peak[...] = jnp.full(peak.shape, 4.0 * NEG_LARGE, jnp.float32)

    def rows_of(buf, p, c):
        return buf[p, :, :, c * HEAD_DIM:(c + 1) * HEAD_DIM].reshape(key_rows, HEAD_DIM)

    def score_step(step, carry):
        p = chip - step

        @pl.when(step > 0)
        def _():
            arrived(k_ref, kbuf, k_recv, p, core)
            to_sibling(kbuf.at[p, core], kbuf, k_fwd, k_recv, p).start()

        arrived(k_ref, kbuf, k_recv, p, other)
        key_pos = (base + 2 * p) * count + lax.broadcasted_iota(jnp.int32, (key_rows, count), 0)
        allowed = (key_pos <= query_pos) & (key_pos >= query_start)
        bias = jnp.where(allowed, 0.0, NEG_LARGE).astype(jnp.float32)
        bias = jnp.concatenate([bias] * GROUP, axis=1)
        for c in range(kv_local):
            scores = dot(rows_of(kbuf, p, c), qs[c], NT) + bias
            probs[c, p] = scores
            peak[c] = jnp.maximum(peak[c], jnp.max(scores, axis=0, keepdims=True))
        return carry

    lax.fori_loop(0, chip + 1, score_step, 0)

    def value_step(step, carry):
        p = chip - step
        arrived(v_ref, vbuf, v_recv, p, core)
        to_sibling(vbuf.at[p, core], vbuf, v_fwd, v_recv, p).start()
        return carry

    lax.fori_loop(1, chip + 1, value_step, 0)

    for c in range(kv_local):
        top = peak[c]

        def exp_step(p, mass, c=c, top=top):
            weights = jnp.exp2((probs[c, p] - top) * (SCALE * math.log2(math.e)))
            probs[c, p] = weights
            return mass + jnp.sum(weights, axis=0, keepdims=True)

        mass = lax.fori_loop(0, chip + 1, exp_step, jnp.zeros((1, columns), jnp.float32))
        inverse = 1.0 / mass

        def norm_step(p, carry, c=c, inverse=inverse):
            probs[c, p] = probs[c, p] * inverse
            return carry

        lax.fori_loop(0, chip + 1, norm_step, 0)

    def far_step(t, carry):
        o = t // chunks
        ch = t % chunks
        w_copy(t).wait()
        og_copy(o, ch).wait_recv()
        project(ogbuf[o - 1, ch], t, False)
        return carry

    lax.fori_loop(chunks, nhead * chunks, far_step, 0)

    def value_wait(p, carry):
        arrived(v_ref, vbuf, v_recv, p, other)
        return carry

    lax.fori_loop(0, chip + 1, value_wait, 0)

    row_pos = me * count + lax.broadcasted_iota(jnp.int32, (count, HEAD_DIM), 0)
    _, answer_first = segment_facts(seq_ref, prompt_ref, row_pos)
    answer = (row_pos >= answer_first).astype(jnp.float32)
    for c in range(kv_local):
        for g in range(GROUP):
            h = c * GROUP + g
            gs[c, g * count:(g + 1) * count, :] = (
                acc[:, h * HEAD_DIM:(h + 1) * HEAD_DIM] * answer
            ).astype(jnp.bfloat16)

    def sib_copy(c, p):
        return remote(
            part.at[c, p, other], sib.at[c, p], sib_send.at[c, p], sib_recv.at[c, p], sibling, head
        )

    def ret_copy(c, p):
        return remote(
            sums.at[c, p], ret.at[c, chip], ret_send.at[c, p], ret_recv.at[c, chip],
            same_core(p), head,
        )

    def combine(c):
        def one(p, carry):
            sib_copy(c, p).wait_recv()
            sums[c, p] = (
                part[c, p, core].astype(jnp.float32) + sib[c, p].astype(jnp.float32)
            ).astype(jnp.bfloat16)
            ret_copy(c, p).start()
            return carry

        lax.fori_loop(0, chip, one, 0)
        sib_copy(c, chip).wait_recv()
        total[c] = part[c, chip, core].astype(jnp.float32) + sib[c, chip].astype(jnp.float32)

    for c in range(kv_local):
        def dprob_step(p, delta, c=c):
            here = dot(rows_of(vbuf, p, c), gs[c], NT)
            dprobs[p] = here
            return delta + jnp.sum(probs[c, p] * here, axis=0, keepdims=True)

        delta = lax.fori_loop(0, chip + 1, dprob_step, jnp.zeros((1, columns), jnp.float32))
        dqt[...] = jnp.zeros(dqt.shape, jnp.float32)

        def grad_step(p, carry, c=c, delta=delta):
            weights = probs[c, p]
            dscores = (weights * (dprobs[p] - delta)).astype(jnp.bfloat16)
            dvalue = dot(weights.astype(jnp.bfloat16), gs[c], NN)
            dkey = dot(dscores, qs[c], NN) * SCALE
            dqt[...] = dqt[...] + dot(rows_of(kbuf, p, c), dscores, TN)
            part[c, p, :, 0] = dkey.astype(jnp.bfloat16).reshape(2, count, HEAD_DIM)
            part[c, p, :, 1] = dvalue.astype(jnp.bfloat16).reshape(2, count, HEAD_DIM)
            sib_copy(c, p).start()
            return carry

        lax.fori_loop(0, chip + 1, grad_step, 0)
        if c > 0:
            combine(c - 1)
        for g in range(GROUP):
            h = c * GROUP + g
            dq_ref[:, h * HEAD_DIM:(h + 1) * HEAD_DIM] = (
                dqt[:, g * count:(g + 1) * count].T * SCALE
            ).astype(jnp.bfloat16)
    combine(kv_local - 1)

    for c in range(kv_local):
        def collect(p, carry, c=c):
            pltpu.make_async_copy(sums.at[c, 0], ret.at[c, p], ret_recv.at[c, p]).wait()
            total[c] = total[c] + ret[c, p].astype(jnp.float32)
            return carry

        lax.fori_loop(chip + 1, chips, collect, 0)
        dk_ref[:, c * HEAD_DIM:(c + 1) * HEAD_DIM] = total[c, 0].astype(jnp.bfloat16)
        dv_ref[:, c * HEAD_DIM:(c + 1) * HEAD_DIM] = total[c, 1].astype(jnp.bfloat16)

    for ch in range(chunks):
        for o in range(1, nhead):
            og_copy(o, ch).wait_send()
    for ref, buf, send, recv, fwd in pairs:
        def sent_direct(p, carry, ref=ref, buf=buf, send=send, recv=recv):
            direct(ref, buf, send, recv, p).wait_send()
            return carry

        lax.fori_loop(chip + 1, chips, sent_direct, 0)

        def sent_on(p, carry, ref=ref, buf=buf, fwd=fwd, recv=recv):
            to_sibling(ref, buf, fwd, recv, p).wait_send()
            return carry

        lax.fori_loop(0, chip + 1, sent_on, 0)
    for c in range(kv_local):
        def sent_part(p, carry, c=c):
            sib_copy(c, p).wait_send()
            return carry

        lax.fori_loop(0, chip + 1, sent_part, 0)

        def sent_sum(p, carry, c=c):
            ret_copy(c, p).wait_send()
            return carry

        lax.fori_loop(0, chip, sent_sum, 0)


def shards(queries, keys, values, out_grad, out_weight, seq_lengths, prompt_lengths):
    nctx = lax.axis_size("ctx")
    nhead = lax.axis_size("head")
    count = queries.shape[0]
    kv_local = keys.shape[1] // HEAD_DIM
    chips = nctx // 4
    features = out_weight.shape[0]
    width = out_grad.shape[1]
    chunk = 512 if width % 512 == 0 else 256
    chunks = width // chunk
    columns = GROUP * count
    bf16, f32 = jnp.bfloat16, jnp.float32
    vmem = pl.BlockSpec(memory_space=pltpu.VMEM)
    smem = pl.BlockSpec(memory_space=pltpu.SMEM)
    dma = pltpu.SemaphoreType.DMA
    far = max(nhead - 1, 1)
    return pl.pallas_call(
        functools.partial(kernel, nctx, nhead, chunk),
        out_shape=(
            jax.ShapeDtypeStruct(queries.shape, bf16),
            jax.ShapeDtypeStruct(keys.shape, bf16),
            jax.ShapeDtypeStruct(values.shape, bf16),
        ),
        in_specs=[vmem, vmem, vmem, vmem, pl.BlockSpec(memory_space=pl.ANY), smem, smem],
        out_specs=(vmem, vmem, vmem),
        scratch_shapes=[
            pltpu.VMEM((nhead * chunks, features, chunk), bf16),
            pltpu.VMEM((far, chunks, count, chunk), bf16),
            pltpu.VMEM((count, features), f32),
            pltpu.VMEM((kv_local, columns, HEAD_DIM), bf16),
            pltpu.VMEM((kv_local, columns, HEAD_DIM), bf16),
            pltpu.VMEM((chips, 2, count, kv_local * HEAD_DIM), bf16),
            pltpu.VMEM((chips, 2, count, kv_local * HEAD_DIM), bf16),
            pltpu.VMEM((kv_local, chips, 2 * count, columns), f32),
            pltpu.VMEM((chips, 2 * count, columns), f32),
            pltpu.VMEM((kv_local, 1, columns), f32),
            pltpu.VMEM((HEAD_DIM, columns), f32),
            pltpu.VMEM((kv_local, chips, 2, 2, count, HEAD_DIM), bf16),
            pltpu.VMEM((kv_local, chips, 2, count, HEAD_DIM), bf16),
            pltpu.VMEM((kv_local, 2, count, HEAD_DIM), f32),
            pltpu.VMEM((kv_local, chips, 2, count, HEAD_DIM), bf16),
            pltpu.VMEM((kv_local, chips, 2, count, HEAD_DIM), bf16),
            dma((nhead * chunks,)),
            dma((far, chunks)),
            dma((far, chunks)),
            dma((chips,)),
            dma((chips,)),
            dma((chips, 2)),
            dma((chips, 2)),
            dma((chips,)),
            dma((chips,)),
            dma((kv_local, chips)),
            dma((kv_local, chips)),
            dma((kv_local, chips)),
            dma((kv_local, chips)),
        ],
        compiler_params=pltpu.CompilerParams(
            collective_id=0, has_side_effects=True, vmem_limit_bytes=60 * 1024 * 1024
        ),
    )(queries, keys, values, out_grad, out_weight, seq_lengths, prompt_lengths)


def solution(mesh):
    return jax.shard_map(
        shards,
        mesh=mesh,
        in_specs=(
            P("ctx", "head"),
            P("ctx", "head"),
            P("ctx", "head"),
            P("ctx", "head"),
            P("head", None),
            P(),
            P(),
        ),
        out_specs=(P("ctx", "head"), P("ctx", "head"), P("ctx", "head")),
        check_vma=False,
    )
```

```python
import functools
import math

import jax
import jax.numpy as jnp
from jax import lax
from jax.experimental import pallas as pl
from jax.experimental.pallas import tpu as pltpu
from jax.sharding import PartitionSpec as P

HEADS_Q = 40
HEADS_KV = 8
HEAD_DIM = 128
GROUP = HEADS_Q // HEADS_KV
SCALE = 1.0 / math.sqrt(HEAD_DIM)
NEG_LARGE = -1e30
NT = (((1,), (1,)), ((), ()))
NN = (((1,), (0,)), ((), ()))
TN = (((0,), (0,)), ((), ()))


def dot(a, b, dims):
    return lax.dot_general(a, b, dims, preferred_element_type=jnp.float32)


def segment_facts(seq_ref, prompt_ref, positions):
    start = jnp.zeros_like(positions)
    first = jnp.zeros_like(positions)
    begin = 0
    for s in range(seq_ref.shape[0]):
        length = seq_ref[s]
        reached = positions >= begin
        start = jnp.where(reached, begin, start)
        first = jnp.where(reached, begin + jnp.minimum(prompt_ref[s], length - 1), first)
        begin = begin + length
    return start, first


def kernel(
    nctx, nhead, chunk,
    q_ref, k_ref, v_ref, og_ref, w_ref, seq_ref, prompt_ref,
    dq_ref, dk_ref, dv_ref,
    wbuf, ogbuf, acc, qs, gs, kbuf, vbuf, probs, peaks, mass, oacc, oacc_t, dqt, part, sib, total, sums, ret,
    w_sem, og_send, og_recv, k_send, v_send, k_recv, v_recv, k_fwd, v_fwd,
    sib_send, sib_recv, ret_send, ret_recv,
):
    count = q_ref.shape[0]
    kv_local = k_ref.shape[1] // HEAD_DIM
    chips = nctx // 4
    features = w_ref.shape[0]
    part_width = og_ref.shape[1]
    chunks = part_width // chunk
    me = lax.axis_index("ctx")
    head = lax.axis_index("head")
    half = me // (nctx // 2)
    base = half * (nctx // 2)
    core = me % 2
    other = 1 - core
    chip = (me - base) // 2
    sibling = me + 1 - 2 * core

    def remote(src, dst, send, recv, ctx, head_at):
        return pltpu.make_async_remote_copy(
            src_ref=src, dst_ref=dst, send_sem=send, recv_sem=recv,
            device_id=(ctx, head_at), device_id_type=pl.DeviceIdType.MESH,
        )

    def same_core(p):
        return base + 2 * p + core

    def w_copy(t):
        column = ((head + t // chunks) % nhead) * part_width + (t % chunks) * chunk
        return pltpu.make_async_copy(
            w_ref.at[:, pl.ds(pl.multiple_of(column, 128), chunk)], wbuf.at[t], w_sem.at[t]
        )

    for t in range(nhead * chunks):
        w_copy(t).start()

    barrier = pltpu.get_barrier_semaphore()

    def greet(ctx, head_at):
        pl.semaphore_signal(
            barrier, inc=1, device_id=(ctx, head_at), device_id_type=pl.DeviceIdType.MESH
        )

    for o in range(1, nhead):
        greet(me, (head + o) % nhead)
    greet(sibling, head)
    for o in range(1, chips):
        greet(same_core((chip + o) % chips), head)
    pl.semaphore_wait(barrier, nhead - 1 + 1 + chips - 1)

    def og_copy(o, ch):
        return remote(
            og_ref.at[:, pl.ds(ch * chunk, chunk)], ogbuf.at[o - 1, ch],
            og_send.at[o - 1, ch], og_recv.at[o - 1, ch], me, (head + nhead - o) % nhead,
        )

    for ch in range(chunks):
        for o in range(1, nhead):
            og_copy(o, ch).start()

    def direct(ref, buf, send, recv, p):
        return remote(ref, buf.at[chip, core], send.at[p], recv.at[chip, core], same_core(p), head)

    def to_sibling(ref, buf, send, recv, p):
        return remote(ref, buf.at[p, core], send.at[p], recv.at[p, core], sibling, head)

    def arrived(ref, buf, recv, p, c):
        pltpu.make_async_copy(ref, buf.at[p, c], recv.at[p, c]).wait()

    pairs = ((k_ref, kbuf, k_send, k_recv, k_fwd), (v_ref, vbuf, v_send, v_recv, v_fwd))
    for ref, buf, send, recv, fwd in pairs:
        to_sibling(ref, buf, fwd, recv, chip).start()

        def send_direct(p, carry, ref=ref, buf=buf, send=send, recv=recv):
            direct(ref, buf, send, recv, p).start()
            return carry

        lax.fori_loop(chip + 1, chips, send_direct, 0)
        buf[chip, core] = ref[...]

    for c in range(kv_local):
        for g in range(GROUP):
            h = c * GROUP + g
            qs[c, g * count:(g + 1) * count, :] = q_ref[:, h * HEAD_DIM:(h + 1) * HEAD_DIM]

    tile = 640 if features % 640 == 0 else HEAD_DIM

    def project(rows, t, first):
        for n in range(0, features, tile):
            here = dot(rows, wbuf[t, n:n + tile, :], NT)
            if first:
                acc[:, n:n + tile] = here
            else:
                acc[:, n:n + tile] = acc[:, n:n + tile] + here

    w_copy(0).wait()
    project(og_ref[:, :chunk], 0, True)

    def own_step(t, carry):
        w_copy(t).wait()
        project(og_ref[:, pl.ds(pl.multiple_of(t * chunk, chunk), chunk)], t, False)
        return carry

    lax.fori_loop(1, chunks, own_step, 0)

    key_rows = 2 * count
    columns = GROUP * count
    query_pos = me * count + lax.broadcasted_iota(jnp.int32, (1, count), 1)
    query_start, _ = segment_facts(seq_ref, prompt_ref, query_pos)
    mass[...] = jnp.zeros(mass.shape, jnp.float32)
    oacc_t[...] = jnp.zeros(oacc_t.shape, jnp.float32)
    factor = SCALE * math.log2(math.e)

    def rows_of(buf, p, c):
        return buf[p, :, :, c * HEAD_DIM:(c + 1) * HEAD_DIM].reshape(key_rows, HEAD_DIM)

    def score_step(step, carry):
        p = chip - step

        @pl.when(step > 0)
        def _():
            arrived(k_ref, kbuf, k_recv, p, core)
            to_sibling(kbuf.at[p, core], kbuf, k_fwd, k_recv, p).start()
            arrived(v_ref, vbuf, v_recv, p, core)
            to_sibling(vbuf.at[p, core], vbuf, v_fwd, v_recv, p).start()

        arrived(k_ref, kbuf, k_recv, p, other)
        key_pos = (base + 2 * p) * count + lax.broadcasted_iota(jnp.int32, (key_rows, count), 0)
        allowed = (key_pos <= query_pos) & (key_pos >= query_start)
        bias = jnp.where(allowed, 0.0, NEG_LARGE).astype(jnp.float32)
        bias = jnp.concatenate([bias] * GROUP, axis=1)
        arrived(v_ref, vbuf, v_recv, p, other)
        tops = []
        for c in range(kv_local):
            scores = dot(rows_of(kbuf, p, c), qs[c], NT) + bias
            before = carry[c]
            top = jnp.maximum(before, jnp.max(scores, axis=0, keepdims=True))
            shrink = jnp.exp2((before - top) * factor)
            weights = jnp.exp2((scores - top) * factor)
            probs[c, p] = weights
            peaks[c, p] = top
            mass[c] = mass[c] * shrink + jnp.sum(weights, axis=0, keepdims=True)
            oacc_t[c] = oacc_t[c] * shrink + dot(
                rows_of(vbuf, p, c), weights.astype(jnp.bfloat16), TN
            )
            tops.append(top)
        return tuple(tops)

    lowest = jnp.full((1, columns), 4.0 * NEG_LARGE, jnp.float32)
    tops = lax.fori_loop(0, chip + 1, score_step, (lowest,) * kv_local)

    for c in range(kv_local):
        inverse = 1.0 / mass[c]

        def scale_step(p, carry, c=c, inverse=inverse):
            peaks[c, p] = jnp.exp2((peaks[c, p] - tops[c]) * factor) * inverse
            return carry

        lax.fori_loop(0, chip + 1, scale_step, 0)
        for g in range(GROUP):
            lanes = slice(g * count, (g + 1) * count)
            oacc[c, lanes, :] = (oacc_t[c, :, lanes] * inverse[:, lanes]).T

    def far_step(t, carry):
        o = t // chunks
        ch = t % chunks
        w_copy(t).wait()
        og_copy(o, ch).wait_recv()
        project(ogbuf[o - 1, ch], t, False)
        return carry

    lax.fori_loop(chunks, nhead * chunks, far_step, 0)

    row_pos = me * count + lax.broadcasted_iota(jnp.int32, (count, HEAD_DIM), 0)
    _, answer_first = segment_facts(seq_ref, prompt_ref, row_pos)
    answer = (row_pos >= answer_first).astype(jnp.float32)
    for c in range(kv_local):
        for g in range(GROUP):
            h = c * GROUP + g
            gs[c, g * count:(g + 1) * count, :] = (
                acc[:, h * HEAD_DIM:(h + 1) * HEAD_DIM] * answer
            ).astype(jnp.bfloat16)

    def sib_copy(c, p):
        return remote(
            part.at[c, p, other], sib.at[c, p], sib_send.at[c, p], sib_recv.at[c, p], sibling, head
        )

    def ret_copy(c, p):
        return remote(
            sums.at[c, p], ret.at[c, chip], ret_send.at[c, p], ret_recv.at[c, chip],
            same_core(p), head,
        )

    def combine(c):
        def one(p, carry):
            sib_copy(c, p).wait_recv()
            sums[c, p] = (
                part[c, p, core].astype(jnp.float32) + sib[c, p].astype(jnp.float32)
            ).astype(jnp.bfloat16)
            ret_copy(c, p).start()
            return carry

        lax.fori_loop(0, chip, one, 0)
        sib_copy(c, chip).wait_recv()
        total[c] = part[c, chip, core].astype(jnp.float32) + sib[c, chip].astype(jnp.float32)

    for c in range(kv_local):
        product = oacc[c] * gs[c].astype(jnp.float32)
        high = product.astype(jnp.bfloat16)
        low = (product - high.astype(jnp.float32)).astype(jnp.bfloat16)
        ones = jnp.ones((16, HEAD_DIM), jnp.bfloat16)
        delta = (dot(ones, high, NT) + dot(ones, low, NT))[:1]
        dqt[...] = jnp.zeros(dqt.shape, jnp.float32)

        def grad_step(p, carry, c=c, delta=delta):
            weights = probs[c, p] * peaks[c, p]
            dvalue = dot(weights.astype(jnp.bfloat16), gs[c], NN)
            dprobs = dot(rows_of(vbuf, p, c), gs[c], NT)
            dscores = (weights * (dprobs - delta)).astype(jnp.bfloat16)
            dkey = dot(dscores, qs[c], NN) * SCALE
            dqt[...] = dqt[...] + dot(rows_of(kbuf, p, c), dscores, TN)
            part[c, p, :, 0] = dkey.astype(jnp.bfloat16).reshape(2, count, HEAD_DIM)
            part[c, p, :, 1] = dvalue.astype(jnp.bfloat16).reshape(2, count, HEAD_DIM)
            sib_copy(c, p).start()
            return carry

        lax.fori_loop(0, chip + 1, grad_step, 0)
        if c > 0:
            combine(c - 1)
        for g in range(GROUP):
            h = c * GROUP + g
            dq_ref[:, h * HEAD_DIM:(h + 1) * HEAD_DIM] = (
                dqt[:, g * count:(g + 1) * count].T * SCALE
            ).astype(jnp.bfloat16)
    combine(kv_local - 1)

    for c in range(kv_local):
        def collect(p, carry, c=c):
            pltpu.make_async_copy(sums.at[c, 0], ret.at[c, p], ret_recv.at[c, p]).wait()
            total[c] = total[c] + ret[c, p].astype(jnp.float32)
            return carry

        lax.fori_loop(chip + 1, chips, collect, 0)
        dk_ref[:, c * HEAD_DIM:(c + 1) * HEAD_DIM] = total[c, 0].astype(jnp.bfloat16)
        dv_ref[:, c * HEAD_DIM:(c + 1) * HEAD_DIM] = total[c, 1].astype(jnp.bfloat16)

    for ch in range(chunks):
        for o in range(1, nhead):
            og_copy(o, ch).wait_send()
    for ref, buf, send, recv, fwd in pairs:
        def sent_direct(p, carry, ref=ref, buf=buf, send=send, recv=recv):
            direct(ref, buf, send, recv, p).wait_send()
            return carry

        lax.fori_loop(chip + 1, chips, sent_direct, 0)

        def sent_on(p, carry, ref=ref, buf=buf, fwd=fwd, recv=recv):
            to_sibling(ref, buf, fwd, recv, p).wait_send()
            return carry

        lax.fori_loop(0, chip + 1, sent_on, 0)
    for c in range(kv_local):
        def sent_part(p, carry, c=c):
            sib_copy(c, p).wait_send()
            return carry

        lax.fori_loop(0, chip + 1, sent_part, 0)

        def sent_sum(p, carry, c=c):
            ret_copy(c, p).wait_send()
            return carry

        lax.fori_loop(0, chip, sent_sum, 0)


def hand_on(*refs):
    sem = refs[-1]
    copies = [pltpu.make_async_copy(refs[i], refs[i + 3], sem.at[i]) for i in range(3)]
    for copy in copies:
        copy.start()
    for copy in copies:
        copy.wait()


def shards(queries, keys, values, out_grad, out_weight, seq_lengths, prompt_lengths):
    nctx = lax.axis_size("ctx")
    nhead = lax.axis_size("head")
    count = queries.shape[0]
    kv_local = keys.shape[1] // HEAD_DIM
    chips = nctx // 4
    features = out_weight.shape[0]
    width = out_grad.shape[1]
    chunk = 512 if width % 512 == 0 else 256
    chunks = width // chunk
    columns = GROUP * count
    bf16, f32 = jnp.bfloat16, jnp.float32
    vmem = pl.BlockSpec(memory_space=pltpu.VMEM)
    smem = pl.BlockSpec(memory_space=pltpu.SMEM)
    dma = pltpu.SemaphoreType.DMA
    far = max(nhead - 1, 1)
    results = pl.pallas_call(
        functools.partial(kernel, nctx, nhead, chunk),
        out_shape=(
            jax.ShapeDtypeStruct(queries.shape, bf16),
            jax.ShapeDtypeStruct(keys.shape, bf16),
            jax.ShapeDtypeStruct(values.shape, bf16),
        ),
        in_specs=[vmem, vmem, vmem, vmem, pl.BlockSpec(memory_space=pl.ANY), smem, smem],
        out_specs=(vmem, vmem, vmem),
        scratch_shapes=[
            pltpu.VMEM((nhead * chunks, features, chunk), bf16),
            pltpu.VMEM((far, chunks, count, chunk), bf16),
            pltpu.VMEM((count, features), f32),
            pltpu.VMEM((kv_local, columns, HEAD_DIM), bf16),
            pltpu.VMEM((kv_local, columns, HEAD_DIM), bf16),
            pltpu.VMEM((chips, 2, count, kv_local * HEAD_DIM), bf16),
            pltpu.VMEM((chips, 2, count, kv_local * HEAD_DIM), bf16),
            pltpu.VMEM((kv_local, chips, 2 * count, columns), f32),
            pltpu.VMEM((kv_local, chips, 1, columns), f32),
            pltpu.VMEM((kv_local, 1, columns), f32),
            pltpu.VMEM((kv_local, columns, HEAD_DIM), f32),
            pltpu.VMEM((kv_local, HEAD_DIM, columns), f32),
            pltpu.VMEM((HEAD_DIM, columns), f32),
            pltpu.VMEM((kv_local, chips, 2, 2, count, HEAD_DIM), bf16),
            pltpu.VMEM((kv_local, chips, 2, count, HEAD_DIM), bf16),
            pltpu.VMEM((kv_local, 2, count, HEAD_DIM), f32),
            pltpu.VMEM((kv_local, chips, 2, count, HEAD_DIM), bf16),
            pltpu.VMEM((kv_local, chips, 2, count, HEAD_DIM), bf16),
            dma((nhead * chunks,)),
            dma((far, chunks)),
            dma((far, chunks)),
            dma((chips,)),
            dma((chips,)),
            dma((chips, 2)),
            dma((chips, 2)),
            dma((chips,)),
            dma((chips,)),
            dma((kv_local, chips)),
            dma((kv_local, chips)),
            dma((kv_local, chips)),
            dma((kv_local, chips)),
        ],
        compiler_params=pltpu.CompilerParams(
            collective_id=0, has_side_effects=True, vmem_limit_bytes=60 * 1024 * 1024
        ),
    )(queries, keys, values, out_grad, out_weight, seq_lengths, prompt_lengths)
    anywhere = pl.BlockSpec(memory_space=pl.ANY)
    return pl.pallas_call(
        hand_on,
        out_shape=tuple(jax.ShapeDtypeStruct(r.shape, r.dtype) for r in results),
        in_specs=[anywhere] * 3,
        out_specs=(anywhere,) * 3,
        scratch_shapes=[dma((3,))],
        compiler_params=pltpu.CompilerParams(vmem_limit_bytes=60 * 1024 * 1024),
    )(*results)


def solution(mesh):
    return jax.shard_map(
        shards,
        mesh=mesh,
        in_specs=(
            P("ctx", "head"),
            P("ctx", "head"),
            P("ctx", "head"),
            P("ctx", "head"),
            P("head", None),
            P(),
            P(),
        ),
        out_specs=(P("ctx", "head"), P("ctx", "head"), P("ctx", "head")),
        check_vma=False,
    )
```

```python
import functools
import math

import jax
import jax.numpy as jnp
from jax import lax
from jax.experimental import pallas as pl
from jax.experimental.pallas import tpu as pltpu
from jax.sharding import PartitionSpec as P

HEADS_Q = 40
HEADS_KV = 8
HEAD_DIM = 128
GROUP = HEADS_Q // HEADS_KV
SCALE = 1.0 / math.sqrt(HEAD_DIM)
NEG_LARGE = -1e30
NT = (((1,), (1,)), ((), ()))
NN = (((1,), (0,)), ((), ()))
TN = (((0,), (0,)), ((), ()))


def dot(a, b, dims):
    return lax.dot_general(a, b, dims, preferred_element_type=jnp.float32)


def segment_facts(seq_ref, prompt_ref, positions):
    start = jnp.zeros_like(positions)
    first = jnp.zeros_like(positions)
    begin = 0
    for s in range(seq_ref.shape[0]):
        length = seq_ref[s]
        reached = positions >= begin
        start = jnp.where(reached, begin, start)
        first = jnp.where(reached, begin + jnp.minimum(prompt_ref[s], length - 1), first)
        begin = begin + length
    return start, first


def kernel(
    nctx, nhead, chunk,
    q_ref, k_ref, v_ref, og_ref, w_ref, seq_ref, prompt_ref,
    dq_ref, dk_ref, dv_ref,
    wbuf, ogbuf, acc, qs, gs, kbuf, vbuf, probs, peaks, top_ref, mass, oacc, oacc_t, dqt, part, sib, total, sums, ret,
    w_sem, og_send, og_recv, k_send, v_send, k_recv, v_recv, k_fwd, v_fwd,
    sib_send, sib_recv, ret_send, ret_recv,
):
    count = q_ref.shape[0]
    kv_local = k_ref.shape[1] // HEAD_DIM
    chips = nctx // 4
    features = w_ref.shape[0]
    part_width = og_ref.shape[1]
    chunks = part_width // chunk
    me = lax.axis_index("ctx")
    head = lax.axis_index("head")
    half = me // (nctx // 2)
    base = half * (nctx // 2)
    core = me % 2
    other = 1 - core
    chip = (me - base) // 2
    sibling = me + 1 - 2 * core

    def remote(src, dst, send, recv, ctx, head_at):
        return pltpu.make_async_remote_copy(
            src_ref=src, dst_ref=dst, send_sem=send, recv_sem=recv,
            device_id=(ctx, head_at), device_id_type=pl.DeviceIdType.MESH,
        )

    def same_core(p):
        return base + 2 * p + core

    def w_copy(t):
        column = ((head + t // chunks) % nhead) * part_width + (t % chunks) * chunk
        return pltpu.make_async_copy(
            w_ref.at[:, pl.ds(pl.multiple_of(column, 128), chunk)], wbuf.at[t], w_sem.at[t]
        )

    for t in range(nhead * chunks):
        w_copy(t).start()

    barrier = pltpu.get_barrier_semaphore()

    def greet(ctx, head_at):
        pl.semaphore_signal(
            barrier, inc=1, device_id=(ctx, head_at), device_id_type=pl.DeviceIdType.MESH
        )

    for o in range(1, nhead):
        greet(me, (head + o) % nhead)
    greet(sibling, head)
    for o in range(1, chips):
        greet(same_core((chip + o) % chips), head)
    pl.semaphore_wait(barrier, nhead - 1 + 1 + chips - 1)

    def og_copy(o, ch):
        return remote(
            og_ref.at[:, pl.ds(ch * chunk, chunk)], ogbuf.at[o - 1, ch],
            og_send.at[o - 1, ch], og_recv.at[o - 1, ch], me, (head + nhead - o) % nhead,
        )

    for ch in range(chunks):
        for o in range(1, nhead):
            og_copy(o, ch).start()

    def direct(ref, buf, send, recv, p):
        return remote(ref, buf.at[chip, core], send.at[p], recv.at[chip, core], same_core(p), head)

    def to_sibling(ref, buf, send, recv, p):
        return remote(ref, buf.at[p, core], send.at[p], recv.at[p, core], sibling, head)

    def arrived(ref, buf, recv, p, c):
        pltpu.make_async_copy(ref, buf.at[p, c], recv.at[p, c]).wait()

    pairs = ((k_ref, kbuf, k_send, k_recv, k_fwd), (v_ref, vbuf, v_send, v_recv, v_fwd))
    for ref, buf, send, recv, fwd in pairs:
        to_sibling(ref, buf, fwd, recv, chip).start()

        def send_direct(p, carry, ref=ref, buf=buf, send=send, recv=recv):
            direct(ref, buf, send, recv, p).start()
            return carry

        lax.fori_loop(chip + 1, chips, send_direct, 0)
        buf[chip, core] = ref[...]

    for c in range(kv_local):
        for g in range(GROUP):
            h = c * GROUP + g
            qs[c, g * count:(g + 1) * count, :] = q_ref[:, h * HEAD_DIM:(h + 1) * HEAD_DIM]

    tile = 640 if features % 640 == 0 else HEAD_DIM

    def project(rows, t, first):
        for n in range(0, features, tile):
            here = dot(rows, wbuf[t, n:n + tile, :], NT)
            if first:
                acc[:, n:n + tile] = here
            else:
                acc[:, n:n + tile] = acc[:, n:n + tile] + here

    key_rows = 2 * count
    columns = GROUP * count
    query_pos = me * count + lax.broadcasted_iota(jnp.int32, (1, count), 1)
    query_start, _ = segment_facts(seq_ref, prompt_ref, query_pos)
    mass[...] = jnp.zeros(mass.shape, jnp.float32)
    oacc_t[...] = jnp.zeros(oacc_t.shape, jnp.float32)
    factor = SCALE * math.log2(math.e)

    def rows_of(buf, p, c):
        return buf[p, :, :, c * HEAD_DIM:(c + 1) * HEAD_DIM].reshape(key_rows, HEAD_DIM)

    def score_step(step):
        p = chip - step

        if not (isinstance(step, int) and step == 0):
            arrived(k_ref, kbuf, k_recv, p, core)
            to_sibling(kbuf.at[p, core], kbuf, k_fwd, k_recv, p).start()
            arrived(v_ref, vbuf, v_recv, p, core)
            to_sibling(vbuf.at[p, core], vbuf, v_fwd, v_recv, p).start()

        arrived(k_ref, kbuf, k_recv, p, other)
        key_pos = (base + 2 * p) * count + lax.broadcasted_iota(jnp.int32, (key_rows, count), 0)
        allowed = (key_pos <= query_pos) & (key_pos >= query_start)
        bias = jnp.where(allowed, 0.0, NEG_LARGE).astype(jnp.float32)
        bias = jnp.concatenate([bias] * GROUP, axis=1)
        arrived(v_ref, vbuf, v_recv, p, other)
        for c in range(kv_local):
            scores = dot(rows_of(kbuf, p, c), qs[c], NT) + bias
            before = top_ref[c]
            top = jnp.maximum(before, jnp.max(scores, axis=0, keepdims=True))
            shrink = jnp.exp2((before - top) * factor)
            weights = jnp.exp2((scores - top) * factor)
            probs[c, p] = weights
            peaks[c, p] = top
            mass[c] = mass[c] * shrink + jnp.sum(weights, axis=0, keepdims=True)
            oacc_t[c] = oacc_t[c] * shrink + dot(
                rows_of(vbuf, p, c), weights.astype(jnp.bfloat16), TN
            )
            top_ref[c] = top

    top_ref[...] = jnp.full(top_ref.shape, 4.0 * NEG_LARGE, jnp.float32)
    score_step(0)

    w_copy(0).wait()
    project(og_ref[:, :chunk], 0, True)

    def own_step(t, carry):
        w_copy(t).wait()
        project(og_ref[:, pl.ds(pl.multiple_of(t * chunk, chunk), chunk)], t, False)
        return carry

    lax.fori_loop(1, chunks, own_step, 0)

    def far_step(t, carry):
        o = t // chunks
        ch = t % chunks
        w_copy(t).wait()
        og_copy(o, ch).wait_recv()
        project(ogbuf[o - 1, ch], t, False)
        return carry

    far = (nhead - 1) * chunks - 1

    def mixed_step(step, carry):
        @pl.when(step <= chip)
        def _():
            score_step(step)

        lax.fori_loop(
            chunks + far * (step - 1) // (chips - 1), chunks + far * step // (chips - 1),
            far_step, 0,
        )
        return carry

    lax.fori_loop(1, chips, mixed_step, 0)

    for c in range(kv_local):
        inverse = 1.0 / mass[c]

        def scale_step(p, carry, c=c, inverse=inverse):
            peaks[c, p] = jnp.exp2((peaks[c, p] - top_ref[c]) * factor) * inverse
            return carry

        lax.fori_loop(0, chip + 1, scale_step, 0)
        for g in range(GROUP):
            lanes = slice(g * count, (g + 1) * count)
            oacc[c, lanes, :] = (oacc_t[c, :, lanes] * inverse[:, lanes]).T

    far_step(chunks + far, 0)

    row_pos = me * count + lax.broadcasted_iota(jnp.int32, (count, HEAD_DIM), 0)
    _, answer_first = segment_facts(seq_ref, prompt_ref, row_pos)
    answer = (row_pos >= answer_first).astype(jnp.float32)
    for c in range(kv_local):
        for g in range(GROUP):
            h = c * GROUP + g
            gs[c, g * count:(g + 1) * count, :] = (
                acc[:, h * HEAD_DIM:(h + 1) * HEAD_DIM] * answer
            ).astype(jnp.bfloat16)

    def sib_copy(c, p):
        return remote(
            part.at[c, p, other], sib.at[c, p], sib_send.at[c, p], sib_recv.at[c, p], sibling, head
        )

    def ret_copy(c, p):
        return remote(
            sums.at[c, p], ret.at[c, chip], ret_send.at[c, p], ret_recv.at[c, chip],
            same_core(p), head,
        )

    def combine(c, p):
        sib_copy(c, p).wait_recv()
        sums[c, p] = (
            part[c, p, core].astype(jnp.float32) + sib[c, p].astype(jnp.float32)
        ).astype(jnp.bfloat16)
        ret_copy(c, p).start()

    together = 2 if kv_local % 2 == 0 else 1
    for start in range(0, kv_local, together):
        heads = range(start, start + together)
        deltas = []
        for c in heads:
            product = oacc[c] * gs[c].astype(jnp.float32)
            high = product.astype(jnp.bfloat16)
            low = (product - high.astype(jnp.float32)).astype(jnp.bfloat16)
            ones = jnp.ones((16, HEAD_DIM), jnp.bfloat16)
            deltas.append((dot(ones, high, NT) + dot(ones, low, NT))[:1])
            dqt[c - start] = jnp.zeros(dqt.shape[1:], jnp.float32)

        def grad_step(p, carry, heads=heads, deltas=deltas, start=start):
            for c in heads:
                weights = probs[c, p] * peaks[c, p]
                dprobs = dot(rows_of(vbuf, p, c), gs[c], NT)
                dvalue = dot(weights.astype(jnp.bfloat16), gs[c], NN)
                dscores = (weights * (dprobs - deltas[c - start])).astype(jnp.bfloat16)
                dkey = dot(dscores, qs[c], NN) * SCALE
                dqt[c - start] = dqt[c - start] + dot(rows_of(kbuf, p, c), dscores, TN)
                part[c, p, :, 0] = dkey.astype(jnp.bfloat16).reshape(2, count, HEAD_DIM)
                part[c, p, :, 1] = dvalue.astype(jnp.bfloat16).reshape(2, count, HEAD_DIM)
                sib_copy(c, p).start()

            @pl.when(p > 0)
            def _():
                for c in heads:
                    combine(c, p - 1)

            return carry

        lax.fori_loop(0, chip + 1, grad_step, 0)
        for c in heads:
            for g in range(GROUP):
                h = c * GROUP + g
                dq_ref[:, h * HEAD_DIM:(h + 1) * HEAD_DIM] = (
                    dqt[c - start, :, g * count:(g + 1) * count].T * SCALE
                ).astype(jnp.bfloat16)

    for c in range(kv_local):
        sib_copy(c, chip).wait_recv()
        total[c] = part[c, chip, core].astype(jnp.float32) + sib[c, chip].astype(jnp.float32)

    for c in range(kv_local):
        def collect(p, carry, c=c):
            pltpu.make_async_copy(sums.at[c, 0], ret.at[c, p], ret_recv.at[c, p]).wait()
            total[c] = total[c] + ret[c, p].astype(jnp.float32)
            return carry

        lax.fori_loop(chip + 1, chips, collect, 0)
        dk_ref[:, c * HEAD_DIM:(c + 1) * HEAD_DIM] = total[c, 0].astype(jnp.bfloat16)
        dv_ref[:, c * HEAD_DIM:(c + 1) * HEAD_DIM] = total[c, 1].astype(jnp.bfloat16)

    for ch in range(chunks):
        for o in range(1, nhead):
            og_copy(o, ch).wait_send()
    for ref, buf, send, recv, fwd in pairs:
        def sent_direct(p, carry, ref=ref, buf=buf, send=send, recv=recv):
            direct(ref, buf, send, recv, p).wait_send()
            return carry

        lax.fori_loop(chip + 1, chips, sent_direct, 0)

        def sent_on(p, carry, ref=ref, buf=buf, fwd=fwd, recv=recv):
            to_sibling(ref, buf, fwd, recv, p).wait_send()
            return carry

        lax.fori_loop(0, chip + 1, sent_on, 0)
    for c in range(kv_local):
        def sent_part(p, carry, c=c):
            sib_copy(c, p).wait_send()
            return carry

        lax.fori_loop(0, chip + 1, sent_part, 0)

        def sent_sum(p, carry, c=c):
            ret_copy(c, p).wait_send()
            return carry

        lax.fori_loop(0, chip, sent_sum, 0)


def hand_on(*refs):
    sources, targets, held = refs[:3], refs[3:6], refs[6:9]
    sem = refs[9]
    loads = [pltpu.make_async_copy(sources[i], held[i], sem.at[i]) for i in range(3)]
    stores = [pltpu.make_async_copy(held[i], targets[i], sem.at[3 + i]) for i in range(3)]
    for load in loads:
        load.start()
    for load, store in zip(loads, stores):
        load.wait()
        store.start()
    for store in stores:
        store.wait()


def shards(queries, keys, values, out_grad, out_weight, seq_lengths, prompt_lengths):
    nctx = lax.axis_size("ctx")
    nhead = lax.axis_size("head")
    count = queries.shape[0]
    kv_local = keys.shape[1] // HEAD_DIM
    chips = nctx // 4
    features = out_weight.shape[0]
    width = out_grad.shape[1]
    chunk = 512 if width % 512 == 0 else 256
    chunks = width // chunk
    columns = GROUP * count
    bf16, f32 = jnp.bfloat16, jnp.float32
    vmem = pl.BlockSpec(memory_space=pltpu.VMEM)
    smem = pl.BlockSpec(memory_space=pltpu.SMEM)
    dma = pltpu.SemaphoreType.DMA
    far = max(nhead - 1, 1)
    results = pl.pallas_call(
        functools.partial(kernel, nctx, nhead, chunk),
        out_shape=(
            jax.ShapeDtypeStruct(queries.shape, bf16),
            jax.ShapeDtypeStruct(keys.shape, bf16),
            jax.ShapeDtypeStruct(values.shape, bf16),
        ),
        in_specs=[vmem, vmem, vmem, vmem, pl.BlockSpec(memory_space=pl.ANY), smem, smem],
        out_specs=(vmem, vmem, vmem),
        scratch_shapes=[
            pltpu.VMEM((nhead * chunks, features, chunk), bf16),
            pltpu.VMEM((far, chunks, count, chunk), bf16),
            pltpu.VMEM((count, features), f32),
            pltpu.VMEM((kv_local, columns, HEAD_DIM), bf16),
            pltpu.VMEM((kv_local, columns, HEAD_DIM), bf16),
            pltpu.VMEM((chips, 2, count, kv_local * HEAD_DIM), bf16),
            pltpu.VMEM((chips, 2, count, kv_local * HEAD_DIM), bf16),
            pltpu.VMEM((kv_local, chips, 2 * count, columns), f32),
            pltpu.VMEM((kv_local, chips, 1, columns), f32),
            pltpu.VMEM((kv_local, 1, columns), f32),
            pltpu.VMEM((kv_local, 1, columns), f32),
            pltpu.VMEM((kv_local, columns, HEAD_DIM), f32),
            pltpu.VMEM((kv_local, HEAD_DIM, columns), f32),
            pltpu.VMEM((2, HEAD_DIM, columns), f32),
            pltpu.VMEM((kv_local, chips, 2, 2, count, HEAD_DIM), bf16),
            pltpu.VMEM((kv_local, chips, 2, count, HEAD_DIM), bf16),
            pltpu.VMEM((kv_local, 2, count, HEAD_DIM), f32),
            pltpu.VMEM((kv_local, chips, 2, count, HEAD_DIM), bf16),
            pltpu.VMEM((kv_local, chips, 2, count, HEAD_DIM), bf16),
            dma((nhead * chunks,)),
            dma((far, chunks)),
            dma((far, chunks)),
            dma((chips,)),
            dma((chips,)),
            dma((chips, 2)),
            dma((chips, 2)),
            dma((chips,)),
            dma((chips,)),
            dma((kv_local, chips)),
            dma((kv_local, chips)),
            dma((kv_local, chips)),
            dma((kv_local, chips)),
        ],
        compiler_params=pltpu.CompilerParams(
            collective_id=0, has_side_effects=True, vmem_limit_bytes=60 * 1024 * 1024
        ),
    )(queries, keys, values, out_grad, out_weight, seq_lengths, prompt_lengths)
    anywhere = pl.BlockSpec(memory_space=pl.ANY)
    return pl.pallas_call(
        hand_on,
        out_shape=tuple(jax.ShapeDtypeStruct(r.shape, r.dtype) for r in results),
        in_specs=[anywhere] * 3,
        out_specs=(anywhere,) * 3,
        scratch_shapes=[pltpu.VMEM(r.shape, r.dtype) for r in results] + [dma((6,))],
        compiler_params=pltpu.CompilerParams(vmem_limit_bytes=60 * 1024 * 1024),
    )(*results)


def solution(mesh):
    return jax.shard_map(
        shards,
        mesh=mesh,
        in_specs=(
            P("ctx", "head"),
            P("ctx", "head"),
            P("ctx", "head"),
            P("ctx", "head"),
            P("head", None),
            P(),
            P(),
        ),
        out_specs=(P("ctx", "head"), P("ctx", "head"), P("ctx", "head")),
        check_vma=False,
    )
```

```python
import functools
import math

import jax
import jax.numpy as jnp
from jax import lax
from jax.experimental import pallas as pl
from jax.experimental.pallas import tpu as pltpu
from jax.sharding import PartitionSpec as P

HEADS_Q = 40
HEADS_KV = 8
HEAD_DIM = 128
GROUP = HEADS_Q // HEADS_KV
SCALE = 1.0 / math.sqrt(HEAD_DIM)
NEG_LARGE = -1e30
NT = (((1,), (1,)), ((), ()))
NN = (((1,), (0,)), ((), ()))
TN = (((0,), (0,)), ((), ()))


def dot(a, b, dims):
    return lax.dot_general(a, b, dims, preferred_element_type=jnp.float32)


def segment_facts(seq_ref, prompt_ref, positions):
    start = jnp.zeros_like(positions)
    first = jnp.zeros_like(positions)
    begin = 0
    for s in range(seq_ref.shape[0]):
        length = seq_ref[s]
        reached = positions >= begin
        start = jnp.where(reached, begin, start)
        first = jnp.where(reached, begin + jnp.minimum(prompt_ref[s], length - 1), first)
        begin = begin + length
    return start, first


def kernel(
    nctx, nhead, chunk,
    q_ref, k_ref, v_ref, og_ref, w_ref, seq_ref, prompt_ref,
    dq_ref, dk_ref, dv_ref,
    wbuf, ogall, acc, qs, gs, gsend, kbuf, vbuf, probs, peaks, top_ref, mass, oacc, oacc_t, dqt, part, sib, total, sums, ret,
    w_sem, og_send, og_recv, ox_send, ox_recv, g_send, g_recv, k_send, v_send, k_recv, v_recv, k_fwd, v_fwd,
    sib_send, sib_recv, ret_send, ret_recv,
):
    count = q_ref.shape[0]
    kv_local = k_ref.shape[1] // HEAD_DIM
    chips = nctx // 4
    features = w_ref.shape[0] // 2
    kv_half = kv_local // 2
    tile = GROUP * HEAD_DIM
    part_width = og_ref.shape[1]
    chunks = part_width // chunk
    me = lax.axis_index("ctx")
    head = lax.axis_index("head")
    half = me // (nctx // 2)
    base = half * (nctx // 2)
    core = me % 2
    other = 1 - core
    chip = (me - base) // 2
    sibling = me + 1 - 2 * core

    def remote(src, dst, send, recv, ctx, head_at):
        return pltpu.make_async_remote_copy(
            src_ref=src, dst_ref=dst, send_sem=send, recv_sem=recv,
            device_id=(ctx, head_at), device_id_type=pl.DeviceIdType.MESH,
        )

    def same_core(p):
        return base + 2 * p + core

    def w_copy(t):
        column = ((head + t // chunks) % nhead) * part_width + (t % chunks) * chunk
        return pltpu.make_async_copy(
            w_ref.at[
                pl.ds(pl.multiple_of(core * features, tile), features),
                pl.ds(pl.multiple_of(column, 128), chunk),
            ],
            wbuf.at[t], w_sem.at[t],
        )

    for t in range(nhead * chunks):
        w_copy(t).start()

    barrier = pltpu.get_barrier_semaphore()

    def greet(ctx, head_at):
        pl.semaphore_signal(
            barrier, inc=1, device_id=(ctx, head_at), device_id_type=pl.DeviceIdType.MESH
        )

    for o in range(1, nhead):
        greet(me, (head + o) % nhead)
    greet(sibling, head)
    for o in range(1, chips):
        greet(same_core((chip + o) % chips), head)
    pl.semaphore_wait(barrier, nhead - 1 + 1 + chips - 1)

    def own_chunk(ch):
        return og_ref.at[:, pl.ds(ch * chunk, chunk)]

    def og_copy(o, ch):
        return remote(
            own_chunk(ch), ogall.at[o, ch, core],
            og_send.at[o - 1, ch], og_recv.at[o - 1, ch], me, (head + nhead - o) % nhead,
        )

    def og_across(src, o, ch):
        return remote(
            src, ogall.at[o, ch, core], ox_send.at[o, ch], ox_recv.at[o, ch], sibling, head
        )

    for ch in range(chunks):
        for o in range(1, nhead):
            og_copy(o, ch).start()
        og_across(own_chunk(ch), 0, ch).start()
        ogall[0, ch, core] = og_ref[:, ch * chunk:(ch + 1) * chunk]

    def direct(ref, buf, send, recv, p):
        return remote(ref, buf.at[chip, core], send.at[p], recv.at[chip, core], same_core(p), head)

    def to_sibling(ref, buf, send, recv, p):
        return remote(ref, buf.at[p, core], send.at[p], recv.at[p, core], sibling, head)

    def arrived(ref, buf, recv, p, c):
        pltpu.make_async_copy(ref, buf.at[p, c], recv.at[p, c]).wait()

    pairs = ((k_ref, kbuf, k_send, k_recv, k_fwd), (v_ref, vbuf, v_send, v_recv, v_fwd))
    for ref, buf, send, recv, fwd in pairs:
        to_sibling(ref, buf, fwd, recv, chip).start()

        def send_direct(p, carry, ref=ref, buf=buf, send=send, recv=recv):
            direct(ref, buf, send, recv, p).start()
            return carry

        lax.fori_loop(chip + 1, chips, send_direct, 0)
        buf[chip, core] = ref[...]

    for c in range(kv_local):
        for g in range(GROUP):
            h = c * GROUP + g
            qs[c, g * count:(g + 1) * count, :] = q_ref[:, h * HEAD_DIM:(h + 1) * HEAD_DIM]

    def project_tile(t, j):
        rows = ogall[t // chunks, t % chunks].reshape(2 * count, chunk)
        return dot(rows, wbuf[t, j * tile:(j + 1) * tile, :], NT)

    def chunk_wait(t):
        w_copy(t).wait()
        og_across(ogall.at[0, 0, core], t // chunks, t % chunks).wait_recv()

    def project(t, carry):
        chunk_wait(t)
        for j in range(kv_half):
            lanes = slice(j * tile, (j + 1) * tile)
            acc[:, lanes] = acc[:, lanes] + project_tile(t, j)
        return carry

    def take_chunk(t):
        o = t // chunks
        ch = t % chunks
        og_copy(o, ch).wait_recv()
        og_across(ogall.at[o, ch, core], o, ch).start()

    key_rows = 2 * count
    columns = GROUP * count
    query_pos = me * count + lax.broadcasted_iota(jnp.int32, (1, count), 1)
    query_start, _ = segment_facts(seq_ref, prompt_ref, query_pos)
    mass[...] = jnp.zeros(mass.shape, jnp.float32)
    oacc_t[...] = jnp.zeros(oacc_t.shape, jnp.float32)
    factor = SCALE * math.log2(math.e)

    def rows_of(buf, p, c):
        return buf[p, :, :, c * HEAD_DIM:(c + 1) * HEAD_DIM].reshape(key_rows, HEAD_DIM)

    def score_step(step):
        p = chip - step

        if not (isinstance(step, int) and step == 0):
            arrived(k_ref, kbuf, k_recv, p, core)
            to_sibling(kbuf.at[p, core], kbuf, k_fwd, k_recv, p).start()
            arrived(v_ref, vbuf, v_recv, p, core)
            to_sibling(vbuf.at[p, core], vbuf, v_fwd, v_recv, p).start()

        arrived(k_ref, kbuf, k_recv, p, other)
        key_pos = (base + 2 * p) * count + lax.broadcasted_iota(jnp.int32, (key_rows, count), 0)
        allowed = (key_pos <= query_pos) & (key_pos >= query_start)
        bias = jnp.where(allowed, 0.0, NEG_LARGE).astype(jnp.float32)
        bias = jnp.concatenate([bias] * GROUP, axis=1)
        arrived(v_ref, vbuf, v_recv, p, other)
        for c in range(kv_local):
            scores = dot(rows_of(kbuf, p, c), qs[c], NT) + bias
            before = top_ref[c]
            top = jnp.maximum(before, jnp.max(scores, axis=0, keepdims=True))
            shrink = jnp.exp2((before - top) * factor)
            weights = jnp.exp2((scores - top) * factor)
            probs[c, p] = weights
            peaks[c, p] = top
            mass[c] = mass[c] * shrink + jnp.sum(weights, axis=0, keepdims=True)
            oacc_t[c] = oacc_t[c] * shrink + dot(
                rows_of(vbuf, p, c), weights.astype(jnp.bfloat16), TN
            )
            top_ref[c] = top

    top_ref[...] = jnp.full(top_ref.shape, 4.0 * NEG_LARGE, jnp.float32)
    score_step(0)

    acc[...] = jnp.zeros(acc.shape, jnp.float32)
    lax.fori_loop(0, chunks - 1, project, 0)

    def far_step(t, carry):
        take_chunk(t)
        return project(t - 1, carry)

    far = (nhead - 1) * chunks - 1

    def mixed_step(step, carry):
        @pl.when(step <= chip)
        def _():
            score_step(step)

        lax.fori_loop(
            chunks + far * (step - 1) // (chips - 1), chunks + far * step // (chips - 1),
            far_step, 0,
        )
        return carry

    lax.fori_loop(1, chips, mixed_step, 0)

    for c in range(kv_local):
        inverse = 1.0 / mass[c]

        def scale_step(p, carry, c=c, inverse=inverse):
            peaks[c, p] = jnp.exp2((peaks[c, p] - top_ref[c]) * factor) * inverse
            return carry

        lax.fori_loop(0, chip + 1, scale_step, 0)
        for g in range(GROUP):
            lanes = slice(g * count, (g + 1) * count)
            oacc[c, lanes, :] = (oacc_t[c, :, lanes] * inverse[:, lanes]).T

    last = nhead * chunks - 1
    far_step(last, 0)
    row_pos = (base + 2 * chip) * count + lax.broadcasted_iota(
        jnp.int32, (2 * count, HEAD_DIM), 0
    )
    _, answer_first = segment_facts(seq_ref, prompt_ref, row_pos)
    answer = (row_pos >= answer_first).astype(jnp.float32)
    answer = jnp.concatenate([answer] * GROUP, axis=1)

    def g_copy(j):
        return remote(
            gsend.at[j], gs.at[core * kv_half + j], g_send.at[j], g_recv.at[j], sibling, head
        )

    chunk_wait(last)
    for j in range(kv_half):
        lanes = slice(j * tile, (j + 1) * tile)
        acc[:, lanes] = (acc[:, lanes] + project_tile(last, j)) * answer
        for g in range(GROUP):
            rows = slice(g * count, (g + 1) * count)
            columns_g = slice(j * tile + g * HEAD_DIM, j * tile + (g + 1) * HEAD_DIM)
            theirs = acc[pl.ds(pl.multiple_of(other * count, count), count), columns_g]
            gsend[j, rows, :] = theirs.astype(jnp.bfloat16)
        g_copy(j).start()
        for g in range(GROUP):
            rows = slice(g * count, (g + 1) * count)
            columns_g = slice(j * tile + g * HEAD_DIM, j * tile + (g + 1) * HEAD_DIM)
            mine = acc[pl.ds(pl.multiple_of(core * count, count), count), columns_g]
            gs[core * kv_half + j, rows, :] = mine.astype(jnp.bfloat16)
    for j in range(kv_half):
        g_copy(j).wait_recv()

    def sib_copy(c, p):
        return remote(
            part.at[c, p, other], sib.at[c, p], sib_send.at[c, p], sib_recv.at[c, p], sibling, head
        )

    def ret_copy(c, p):
        return remote(
            sums.at[c, p], ret.at[c, chip], ret_send.at[c, p], ret_recv.at[c, chip],
            same_core(p), head,
        )

    def combine(c, p):
        sib_copy(c, p).wait_recv()
        sums[c, p] = (
            part[c, p, core].astype(jnp.float32) + sib[c, p].astype(jnp.float32)
        ).astype(jnp.bfloat16)
        ret_copy(c, p).start()

    together = 2 if kv_local % 2 == 0 else 1
    for start in range(0, kv_local, together):
        heads = range(start, start + together)
        deltas = []
        for c in heads:
            product = oacc[c] * gs[c].astype(jnp.float32)
            high = product.astype(jnp.bfloat16)
            low = (product - high.astype(jnp.float32)).astype(jnp.bfloat16)
            ones = jnp.ones((16, HEAD_DIM), jnp.bfloat16)
            deltas.append((dot(ones, high, NT) + dot(ones, low, NT))[:1])
            dqt[c - start] = jnp.zeros(dqt.shape[1:], jnp.float32)

        def grad_step(p, carry, heads=heads, deltas=deltas, start=start):
            for c in heads:
                weights = probs[c, p] * peaks[c, p]
                dprobs = dot(rows_of(vbuf, p, c), gs[c], NT)
                dvalue = dot(weights.astype(jnp.bfloat16), gs[c], NN)
                dscores = (weights * (dprobs - deltas[c - start])).astype(jnp.bfloat16)
                dkey = dot(dscores, qs[c], NN) * SCALE
                dqt[c - start] = dqt[c - start] + dot(rows_of(kbuf, p, c), dscores, TN)
                part[c, p, :, 0] = dkey.astype(jnp.bfloat16).reshape(2, count, HEAD_DIM)
                part[c, p, :, 1] = dvalue.astype(jnp.bfloat16).reshape(2, count, HEAD_DIM)
                sib_copy(c, p).start()

            @pl.when(p > 0)
            def _():
                for c in heads:
                    combine(c, p - 1)

            return carry

        lax.fori_loop(0, chip + 1, grad_step, 0)
        for c in heads:
            for g in range(GROUP):
                h = c * GROUP + g
                dq_ref[:, h * HEAD_DIM:(h + 1) * HEAD_DIM] = (
                    dqt[c - start, :, g * count:(g + 1) * count].T * SCALE
                ).astype(jnp.bfloat16)

    for c in range(kv_local):
        sib_copy(c, chip).wait_recv()
        total[c] = part[c, chip, core].astype(jnp.float32) + sib[c, chip].astype(jnp.float32)

    for c in range(kv_local):
        def collect(p, carry, c=c):
            pltpu.make_async_copy(sums.at[c, 0], ret.at[c, p], ret_recv.at[c, p]).wait()
            total[c] = total[c] + ret[c, p].astype(jnp.float32)
            return carry

        lax.fori_loop(chip + 1, chips, collect, 0)
        dk_ref[:, c * HEAD_DIM:(c + 1) * HEAD_DIM] = total[c, 0].astype(jnp.bfloat16)
        dv_ref[:, c * HEAD_DIM:(c + 1) * HEAD_DIM] = total[c, 1].astype(jnp.bfloat16)

    for ch in range(chunks):
        for o in range(1, nhead):
            og_copy(o, ch).wait_send()
        for o in range(nhead):
            og_across(own_chunk(ch), o, ch).wait_send()
    for j in range(kv_half):
        g_copy(j).wait_send()
    for ref, buf, send, recv, fwd in pairs:
        def sent_direct(p, carry, ref=ref, buf=buf, send=send, recv=recv):
            direct(ref, buf, send, recv, p).wait_send()
            return carry

        lax.fori_loop(chip + 1, chips, sent_direct, 0)

        def sent_on(p, carry, ref=ref, buf=buf, fwd=fwd, recv=recv):
            to_sibling(ref, buf, fwd, recv, p).wait_send()
            return carry

        lax.fori_loop(0, chip + 1, sent_on, 0)
    for c in range(kv_local):
        def sent_part(p, carry, c=c):
            sib_copy(c, p).wait_send()
            return carry

        lax.fori_loop(0, chip + 1, sent_part, 0)

        def sent_sum(p, carry, c=c):
            ret_copy(c, p).wait_send()
            return carry

        lax.fori_loop(0, chip, sent_sum, 0)


def hand_on(*refs):
    sources, targets, held = refs[:3], refs[3:6], refs[6:9]
    sem = refs[9]
    loads = [pltpu.make_async_copy(sources[i], held[i], sem.at[i]) for i in range(3)]
    stores = [pltpu.make_async_copy(held[i], targets[i], sem.at[3 + i]) for i in range(3)]
    for load in loads:
        load.start()
    for load, store in zip(loads, stores):
        load.wait()
        store.start()
    for store in stores:
        store.wait()


def shards(queries, keys, values, out_grad, out_weight, seq_lengths, prompt_lengths):
    nctx = lax.axis_size("ctx")
    nhead = lax.axis_size("head")
    count = queries.shape[0]
    kv_local = keys.shape[1] // HEAD_DIM
    chips = nctx // 4
    features = out_weight.shape[0] // 2
    kv_half = kv_local // 2
    width = out_grad.shape[1]
    chunk = 512 if width % 512 == 0 else 256
    chunks = width // chunk
    columns = GROUP * count
    bf16, f32 = jnp.bfloat16, jnp.float32
    vmem = pl.BlockSpec(memory_space=pltpu.VMEM)
    smem = pl.BlockSpec(memory_space=pltpu.SMEM)
    dma = pltpu.SemaphoreType.DMA
    far = max(nhead - 1, 1)
    results = pl.pallas_call(
        functools.partial(kernel, nctx, nhead, chunk),
        out_shape=(
            jax.ShapeDtypeStruct(queries.shape, bf16),
            jax.ShapeDtypeStruct(keys.shape, bf16),
            jax.ShapeDtypeStruct(values.shape, bf16),
        ),
        in_specs=[vmem, vmem, vmem, vmem, pl.BlockSpec(memory_space=pl.ANY), smem, smem],
        out_specs=(vmem, vmem, vmem),
        scratch_shapes=[
            pltpu.VMEM((nhead * chunks, features, chunk), bf16),
            pltpu.VMEM((nhead, chunks, 2, count, chunk), bf16),
            pltpu.VMEM((2 * count, features), f32),
            pltpu.VMEM((kv_local, columns, HEAD_DIM), bf16),
            pltpu.VMEM((kv_local, columns, HEAD_DIM), bf16),
            pltpu.VMEM((kv_half, columns, HEAD_DIM), bf16),
            pltpu.VMEM((chips, 2, count, kv_local * HEAD_DIM), bf16),
            pltpu.VMEM((chips, 2, count, kv_local * HEAD_DIM), bf16),
            pltpu.VMEM((kv_local, chips, 2 * count, columns), f32),
            pltpu.VMEM((kv_local, chips, 1, columns), f32),
            pltpu.VMEM((kv_local, 1, columns), f32),
            pltpu.VMEM((kv_local, 1, columns), f32),
            pltpu.VMEM((kv_local, columns, HEAD_DIM), f32),
            pltpu.VMEM((kv_local, HEAD_DIM, columns), f32),
            pltpu.VMEM((2, HEAD_DIM, columns), f32),
            pltpu.VMEM((kv_local, chips, 2, 2, count, HEAD_DIM), bf16),
            pltpu.VMEM((kv_local, chips, 2, count, HEAD_DIM), bf16),
            pltpu.VMEM((kv_local, 2, count, HEAD_DIM), f32),
            pltpu.VMEM((kv_local, chips, 2, count, HEAD_DIM), bf16),
            pltpu.VMEM((kv_local, chips, 2, count, HEAD_DIM), bf16),
            dma((nhead * chunks,)),
            dma((far, chunks)),
            dma((far, chunks)),
            dma((nhead, chunks)),
            dma((nhead, chunks)),
            dma((kv_half,)),
            dma((kv_half,)),
            dma((chips,)),
            dma((chips,)),
            dma((chips, 2)),
            dma((chips, 2)),
            dma((chips,)),
            dma((chips,)),
            dma((kv_local, chips)),
            dma((kv_local, chips)),
            dma((kv_local, chips)),
            dma((kv_local, chips)),
        ],
        compiler_params=pltpu.CompilerParams(
            collective_id=0, has_side_effects=True, vmem_limit_bytes=60 * 1024 * 1024
        ),
    )(queries, keys, values, out_grad, out_weight, seq_lengths, prompt_lengths)
    anywhere = pl.BlockSpec(memory_space=pl.ANY)
    return pl.pallas_call(
        hand_on,
        out_shape=tuple(jax.ShapeDtypeStruct(r.shape, r.dtype) for r in results),
        in_specs=[anywhere] * 3,
        out_specs=(anywhere,) * 3,
        scratch_shapes=[pltpu.VMEM(r.shape, r.dtype) for r in results] + [dma((6,))],
        compiler_params=pltpu.CompilerParams(vmem_limit_bytes=60 * 1024 * 1024),
    )(*results)


def solution(mesh):
    return jax.shard_map(
        shards,
        mesh=mesh,
        in_specs=(
            P("ctx", "head"),
            P("ctx", "head"),
            P("ctx", "head"),
            P("ctx", "head"),
            P("head", None),
            P(),
            P(),
        ),
        out_specs=(P("ctx", "head"), P("ctx", "head"), P("ctx", "head")),
        check_vma=False,
    )
```

```python
import functools
import math

import jax
import jax.numpy as jnp
from jax import lax
from jax.experimental import pallas as pl
from jax.experimental.pallas import tpu as pltpu
from jax.sharding import PartitionSpec as P

HEADS_Q = 40
HEADS_KV = 8
HEAD_DIM = 128
GROUP = HEADS_Q // HEADS_KV
SCALE = 1.0 / math.sqrt(HEAD_DIM)
NEG_LARGE = -1e30
NT = (((1,), (1,)), ((), ()))
NN = (((1,), (0,)), ((), ()))
TN = (((0,), (0,)), ((), ()))


def dot(a, b, dims):
    return lax.dot_general(a, b, dims, preferred_element_type=jnp.float32)


def segment_facts(seq_ref, prompt_ref, positions):
    start = jnp.zeros_like(positions)
    first = jnp.zeros_like(positions)
    begin = 0
    for s in range(seq_ref.shape[0]):
        length = seq_ref[s]
        reached = positions >= begin
        start = jnp.where(reached, begin, start)
        first = jnp.where(reached, begin + jnp.minimum(prompt_ref[s], length - 1), first)
        begin = begin + length
    return start, first


def kernel(
    nctx, nhead, chunk,
    q_ref, k_ref, v_ref, og_ref, w_ref, seq_ref, prompt_ref,
    dq_ref, dk_ref, dv_ref,
    wbuf, ogall, acc, qs, gs, gsend, kbuf, vbuf, probs, peaks, top_ref, mass, dprobs, dqt, part, sib, total, sums, ret,
    w_sem, og_send, og_recv, ox_send, ox_recv, g_send, g_recv, k_send, v_send, k_recv, v_recv, k_fwd, v_fwd,
    sib_send, sib_recv, ret_send, ret_recv,
):
    count = q_ref.shape[0]
    kv_local = k_ref.shape[1] // HEAD_DIM
    chips = nctx // 4
    features = w_ref.shape[0] // 2
    kv_half = kv_local // 2
    tile = GROUP * HEAD_DIM
    part_width = og_ref.shape[1]
    chunks = part_width // chunk
    me = lax.axis_index("ctx")
    head = lax.axis_index("head")
    half = me // (nctx // 2)
    base = half * (nctx // 2)
    core = me % 2
    other = 1 - core
    chip = (me - base) // 2
    sibling = me + 1 - 2 * core

    def remote(src, dst, send, recv, ctx, head_at):
        return pltpu.make_async_remote_copy(
            src_ref=src, dst_ref=dst, send_sem=send, recv_sem=recv,
            device_id=(ctx, head_at), device_id_type=pl.DeviceIdType.MESH,
        )

    def same_core(p):
        return base + 2 * p + core

    def w_copy(t):
        column = ((head + t // chunks) % nhead) * part_width + (t % chunks) * chunk
        return pltpu.make_async_copy(
            w_ref.at[
                pl.ds(pl.multiple_of(core * features, tile), features),
                pl.ds(pl.multiple_of(column, 128), chunk),
            ],
            wbuf.at[t], w_sem.at[t],
        )

    for t in range(nhead * chunks):
        w_copy(t).start()

    barrier = pltpu.get_barrier_semaphore()

    def greet(ctx, head_at):
        pl.semaphore_signal(
            barrier, inc=1, device_id=(ctx, head_at), device_id_type=pl.DeviceIdType.MESH
        )

    for o in range(1, nhead):
        greet(me, (head + o) % nhead)
    greet(sibling, head)
    for o in range(1, chips):
        greet(same_core((chip + o) % chips), head)
    pl.semaphore_wait(barrier, nhead - 1 + 1 + chips - 1)

    def own_chunk(ch):
        return og_ref.at[:, pl.ds(ch * chunk, chunk)]

    def og_copy(o, ch):
        return remote(
            own_chunk(ch), ogall.at[o, ch, core],
            og_send.at[o - 1, ch], og_recv.at[o - 1, ch], me, (head + nhead - o) % nhead,
        )

    def og_across(src, o, ch):
        return remote(
            src, ogall.at[o, ch, core], ox_send.at[o, ch], ox_recv.at[o, ch], sibling, head
        )

    for ch in range(chunks):
        for o in range(1, nhead):
            og_copy(o, ch).start()
        og_across(own_chunk(ch), 0, ch).start()
        ogall[0, ch, core] = og_ref[:, ch * chunk:(ch + 1) * chunk]

    def direct(ref, buf, send, recv, p):
        return remote(ref, buf.at[chip, core], send.at[p], recv.at[chip, core], same_core(p), head)

    def to_sibling(ref, buf, send, recv, p):
        return remote(ref, buf.at[p, core], send.at[p], recv.at[p, core], sibling, head)

    def arrived(ref, buf, recv, p, c):
        pltpu.make_async_copy(ref, buf.at[p, c], recv.at[p, c]).wait()

    pairs = ((k_ref, kbuf, k_send, k_recv, k_fwd), (v_ref, vbuf, v_send, v_recv, v_fwd))
    for ref, buf, send, recv, fwd in pairs:
        to_sibling(ref, buf, fwd, recv, chip).start()

        def send_direct(p, carry, ref=ref, buf=buf, send=send, recv=recv):
            direct(ref, buf, send, recv, p).start()
            return carry

        lax.fori_loop(chip + 1, chips, send_direct, 0)
        buf[chip, core] = ref[...]

    for c in range(kv_local):
        for g in range(GROUP):
            h = c * GROUP + g
            qs[c, g * count:(g + 1) * count, :] = q_ref[:, h * HEAD_DIM:(h + 1) * HEAD_DIM]

    def project_tile(t, j):
        rows = ogall[t // chunks, t % chunks].reshape(2 * count, chunk)
        return dot(rows, wbuf[t, j * tile:(j + 1) * tile, :], NT)

    def chunk_wait(t):
        w_copy(t).wait()
        og_across(ogall.at[0, 0, core], t // chunks, t % chunks).wait_recv()

    def project(t, carry):
        chunk_wait(t)
        for j in range(kv_half):
            lanes = slice(j * tile, (j + 1) * tile)
            acc[:, lanes] = acc[:, lanes] + project_tile(t, j)
        return carry

    def take_chunk(t):
        o = t // chunks
        ch = t % chunks
        og_copy(o, ch).wait_recv()
        og_across(ogall.at[o, ch, core], o, ch).start()

    key_rows = 2 * count
    columns = GROUP * count
    query_pos = me * count + lax.broadcasted_iota(jnp.int32, (1, count), 1)
    query_start, _ = segment_facts(seq_ref, prompt_ref, query_pos)
    mass[...] = jnp.zeros(mass.shape, jnp.float32)
    factor = SCALE * math.log2(math.e)

    def rows_of(buf, p, c):
        return buf[p, :, :, c * HEAD_DIM:(c + 1) * HEAD_DIM].reshape(key_rows, HEAD_DIM)

    def score_step(step):
        p = chip - step

        if not (isinstance(step, int) and step == 0):
            arrived(k_ref, kbuf, k_recv, p, core)
            to_sibling(kbuf.at[p, core], kbuf, k_fwd, k_recv, p).start()

        arrived(k_ref, kbuf, k_recv, p, other)
        key_pos = (base + 2 * p) * count + lax.broadcasted_iota(jnp.int32, (key_rows, count), 0)
        allowed = (key_pos <= query_pos) & (key_pos >= query_start)
        bias = jnp.where(allowed, 0.0, NEG_LARGE).astype(jnp.float32)
        bias = jnp.concatenate([bias] * GROUP, axis=1)
        for c in range(kv_local):
            scores = dot(rows_of(kbuf, p, c), qs[c], NT) + bias
            before = top_ref[c]
            top = jnp.maximum(before, jnp.max(scores, axis=0, keepdims=True))
            shrink = jnp.exp2((before - top) * factor)
            weights = jnp.exp2((scores - top) * factor)
            probs[c, p] = weights
            peaks[c, p] = top
            mass[c] = mass[c] * shrink + jnp.sum(weights, axis=0, keepdims=True)
            top_ref[c] = top

    top_ref[...] = jnp.full(top_ref.shape, 4.0 * NEG_LARGE, jnp.float32)
    score_step(0)

    acc[...] = jnp.zeros(acc.shape, jnp.float32)
    lax.fori_loop(0, chunks - 1, project, 0)

    def far_step(t, carry):
        take_chunk(t)
        return project(t - 1, carry)

    far = (nhead - 1) * chunks - 1

    def mixed_step(step, carry):
        @pl.when(step <= chip)
        def _():
            score_step(step)

        lax.fori_loop(
            chunks + far * (step - 1) // (chips - 1), chunks + far * step // (chips - 1),
            far_step, 0,
        )
        return carry

    lax.fori_loop(1, chips, mixed_step, 0)

    for c in range(kv_local):
        inverse = 1.0 / mass[c]

        def scale_step(p, carry, c=c, inverse=inverse):
            peaks[c, p] = jnp.exp2((peaks[c, p] - top_ref[c]) * factor) * inverse
            return carry

        lax.fori_loop(0, chip + 1, scale_step, 0)
    def value_step(step, carry):
        p = chip - step
        arrived(v_ref, vbuf, v_recv, p, core)
        to_sibling(vbuf.at[p, core], vbuf, v_fwd, v_recv, p).start()
        return carry

    lax.fori_loop(1, chip + 1, value_step, 0)

    last = nhead * chunks - 1
    far_step(last, 0)
    row_pos = (base + 2 * chip) * count + lax.broadcasted_iota(
        jnp.int32, (2 * count, HEAD_DIM), 0
    )
    _, answer_first = segment_facts(seq_ref, prompt_ref, row_pos)
    answer = (row_pos >= answer_first).astype(jnp.float32)
    answer = jnp.concatenate([answer] * GROUP, axis=1)

    def g_copy(j):
        return remote(
            gsend.at[j], gs.at[core * kv_half + j], g_send.at[j], g_recv.at[j], sibling, head
        )

    chunk_wait(last)
    for j in range(kv_half):
        lanes = slice(j * tile, (j + 1) * tile)
        acc[:, lanes] = (acc[:, lanes] + project_tile(last, j)) * answer
        for g in range(GROUP):
            rows = slice(g * count, (g + 1) * count)
            columns_g = slice(j * tile + g * HEAD_DIM, j * tile + (g + 1) * HEAD_DIM)
            theirs = acc[pl.ds(pl.multiple_of(other * count, count), count), columns_g]
            gsend[j, rows, :] = theirs.astype(jnp.bfloat16)
        g_copy(j).start()
        for g in range(GROUP):
            rows = slice(g * count, (g + 1) * count)
            columns_g = slice(j * tile + g * HEAD_DIM, j * tile + (g + 1) * HEAD_DIM)
            mine = acc[pl.ds(pl.multiple_of(core * count, count), count), columns_g]
            gs[core * kv_half + j, rows, :] = mine.astype(jnp.bfloat16)
    for j in range(kv_half):
        g_copy(j).wait_recv()

    def sib_copy(c, p):
        return remote(
            part.at[c, p, other], sib.at[c, p], sib_send.at[c, p], sib_recv.at[c, p], sibling, head
        )

    def ret_copy(c, p):
        return remote(
            sums.at[c, p], ret.at[c, chip], ret_send.at[c, p], ret_recv.at[c, chip],
            same_core(p), head,
        )

    def combine(c, p):
        sib_copy(c, p).wait_recv()
        sums[c, p] = (
            part[c, p, core].astype(jnp.float32) + sib[c, p].astype(jnp.float32)
        ).astype(jnp.bfloat16)
        ret_copy(c, p).start()

    together = 2 if kv_local % 2 == 0 else 1
    for start in range(0, kv_local, together):
        heads = range(start, start + together)
        for c in heads:
            dqt[c - start] = jnp.zeros(dqt.shape[1:], jnp.float32)

        def delta_step(p, deltas, heads=heads, start=start):
            if start == 0:
                arrived(v_ref, vbuf, v_recv, p, other)
            found = []
            for c in heads:
                here = dot(rows_of(vbuf, p, c), gs[c], NT)
                dprobs[c - start, p] = here
                found.append(
                    deltas[c - start]
                    + jnp.sum(probs[c, p] * here, axis=0, keepdims=True) * peaks[c, p]
                )
            return tuple(found)

        deltas = lax.fori_loop(
            0, chip + 1, delta_step, (jnp.zeros((1, columns), jnp.float32),) * together
        )

        def grad_step(p, carry, heads=heads, deltas=deltas, start=start):
            for c in heads:
                weights = probs[c, p] * peaks[c, p]
                dvalue = dot(weights.astype(jnp.bfloat16), gs[c], NN)
                dscores = (weights * (dprobs[c - start, p] - deltas[c - start])).astype(jnp.bfloat16)
                dkey = dot(dscores, qs[c], NN) * SCALE
                dqt[c - start] = dqt[c - start] + dot(rows_of(kbuf, p, c), dscores, TN)
                part[c, p, :, 0] = dkey.astype(jnp.bfloat16).reshape(2, count, HEAD_DIM)
                part[c, p, :, 1] = dvalue.astype(jnp.bfloat16).reshape(2, count, HEAD_DIM)
                sib_copy(c, p).start()

            @pl.when(p > 0)
            def _():
                for c in heads:
                    combine(c, p - 1)

            return carry

        lax.fori_loop(0, chip + 1, grad_step, 0)
        for c in heads:
            for g in range(GROUP):
                h = c * GROUP + g
                dq_ref[:, h * HEAD_DIM:(h + 1) * HEAD_DIM] = (
                    dqt[c - start, :, g * count:(g + 1) * count].T * SCALE
                ).astype(jnp.bfloat16)

    for c in range(kv_local):
        sib_copy(c, chip).wait_recv()
        total[c] = part[c, chip, core].astype(jnp.float32) + sib[c, chip].astype(jnp.float32)

    for c in range(kv_local):
        def collect(p, carry, c=c):
            pltpu.make_async_copy(sums.at[c, 0], ret.at[c, p], ret_recv.at[c, p]).wait()
            total[c] = total[c] + ret[c, p].astype(jnp.float32)
            return carry

        lax.fori_loop(chip + 1, chips, collect, 0)
        dk_ref[:, c * HEAD_DIM:(c + 1) * HEAD_DIM] = total[c, 0].astype(jnp.bfloat16)
        dv_ref[:, c * HEAD_DIM:(c + 1) * HEAD_DIM] = total[c, 1].astype(jnp.bfloat16)

    for ch in range(chunks):
        for o in range(1, nhead):
            og_copy(o, ch).wait_send()
        for o in range(nhead):
            og_across(own_chunk(ch), o, ch).wait_send()
    for j in range(kv_half):
        g_copy(j).wait_send()
    for ref, buf, send, recv, fwd in pairs:
        def sent_direct(p, carry, ref=ref, buf=buf, send=send, recv=recv):
            direct(ref, buf, send, recv, p).wait_send()
            return carry

        lax.fori_loop(chip + 1, chips, sent_direct, 0)

        def sent_on(p, carry, ref=ref, buf=buf, fwd=fwd, recv=recv):
            to_sibling(ref, buf, fwd, recv, p).wait_send()
            return carry

        lax.fori_loop(0, chip + 1, sent_on, 0)
    for c in range(kv_local):
        def sent_part(p, carry, c=c):
            sib_copy(c, p).wait_send()
            return carry

        lax.fori_loop(0, chip + 1, sent_part, 0)

        def sent_sum(p, carry, c=c):
            ret_copy(c, p).wait_send()
            return carry

        lax.fori_loop(0, chip, sent_sum, 0)


def hand_on(*refs):
    sources, targets, held = refs[:3], refs[3:6], refs[6:9]
    sem = refs[9]
    loads = [pltpu.make_async_copy(sources[i], held[i], sem.at[i]) for i in range(3)]
    stores = [pltpu.make_async_copy(held[i], targets[i], sem.at[3 + i]) for i in range(3)]
    for load in loads:
        load.start()
    for load, store in zip(loads, stores):
        load.wait()
        store.start()
    for store in stores:
        store.wait()


def shards(queries, keys, values, out_grad, out_weight, seq_lengths, prompt_lengths):
    nctx = lax.axis_size("ctx")
    nhead = lax.axis_size("head")
    count = queries.shape[0]
    kv_local = keys.shape[1] // HEAD_DIM
    chips = nctx // 4
    features = out_weight.shape[0] // 2
    kv_half = kv_local // 2
    width = out_grad.shape[1]
    chunk = 512 if width % 512 == 0 else 256
    chunks = width // chunk
    columns = GROUP * count
    bf16, f32 = jnp.bfloat16, jnp.float32
    vmem = pl.BlockSpec(memory_space=pltpu.VMEM)
    smem = pl.BlockSpec(memory_space=pltpu.SMEM)
    dma = pltpu.SemaphoreType.DMA
    far = max(nhead - 1, 1)
    results = pl.pallas_call(
        functools.partial(kernel, nctx, nhead, chunk),
        out_shape=(
            jax.ShapeDtypeStruct(queries.shape, bf16),
            jax.ShapeDtypeStruct(keys.shape, bf16),
            jax.ShapeDtypeStruct(values.shape, bf16),
        ),
        in_specs=[vmem, vmem, vmem, vmem, pl.BlockSpec(memory_space=pl.ANY), smem, smem],
        out_specs=(vmem, vmem, vmem),
        scratch_shapes=[
            pltpu.VMEM((nhead * chunks, features, chunk), bf16),
            pltpu.VMEM((nhead, chunks, 2, count, chunk), bf16),
            pltpu.VMEM((2 * count, features), f32),
            pltpu.VMEM((kv_local, columns, HEAD_DIM), bf16),
            pltpu.VMEM((kv_local, columns, HEAD_DIM), bf16),
            pltpu.VMEM((kv_half, columns, HEAD_DIM), bf16),
            pltpu.VMEM((chips, 2, count, kv_local * HEAD_DIM), bf16),
            pltpu.VMEM((chips, 2, count, kv_local * HEAD_DIM), bf16),
            pltpu.VMEM((kv_local, chips, 2 * count, columns), f32),
            pltpu.VMEM((kv_local, chips, 1, columns), f32),
            pltpu.VMEM((kv_local, 1, columns), f32),
            pltpu.VMEM((kv_local, 1, columns), f32),
            pltpu.VMEM((2, chips, 2 * count, columns), f32),
            pltpu.VMEM((2, HEAD_DIM, columns), f32),
            pltpu.VMEM((kv_local, chips, 2, 2, count, HEAD_DIM), bf16),
            pltpu.VMEM((kv_local, chips, 2, count, HEAD_DIM), bf16),
            pltpu.VMEM((kv_local, 2, count, HEAD_DIM), f32),
            pltpu.VMEM((kv_local, chips, 2, count, HEAD_DIM), bf16),
            pltpu.VMEM((kv_local, chips, 2, count, HEAD_DIM), bf16),
            dma((nhead * chunks,)),
            dma((far, chunks)),
            dma((far, chunks)),
            dma((nhead, chunks)),
            dma((nhead, chunks)),
            dma((kv_half,)),
            dma((kv_half,)),
            dma((chips,)),
            dma((chips,)),
            dma((chips, 2)),
            dma((chips, 2)),
            dma((chips,)),
            dma((chips,)),
            dma((kv_local, chips)),
            dma((kv_local, chips)),
            dma((kv_local, chips)),
            dma((kv_local, chips)),
        ],
        compiler_params=pltpu.CompilerParams(
            collective_id=0, has_side_effects=True, vmem_limit_bytes=60 * 1024 * 1024
        ),
    )(queries, keys, values, out_grad, out_weight, seq_lengths, prompt_lengths)
    anywhere = pl.BlockSpec(memory_space=pl.ANY)
    return pl.pallas_call(
        hand_on,
        out_shape=tuple(jax.ShapeDtypeStruct(r.shape, r.dtype) for r in results),
        in_specs=[anywhere] * 3,
        out_specs=(anywhere,) * 3,
        scratch_shapes=[pltpu.VMEM(r.shape, r.dtype) for r in results] + [dma((6,))],
        compiler_params=pltpu.CompilerParams(vmem_limit_bytes=60 * 1024 * 1024),
    )(*results)


def solution(mesh):
    return jax.shard_map(
        shards,
        mesh=mesh,
        in_specs=(
            P("ctx", "head"),
            P("ctx", "head"),
            P("ctx", "head"),
            P("ctx", "head"),
            P("head", None),
            P(),
            P(),
        ),
        out_specs=(P("ctx", "head"), P("ctx", "head"), P("ctx", "head")),
        check_vma=False,
    )
```

```python
import functools
import math

import jax
import jax.numpy as jnp
from jax import lax
from jax.experimental import pallas as pl
from jax.experimental.pallas import tpu as pltpu
from jax.sharding import PartitionSpec as P

HEADS_Q = 40
HEADS_KV = 8
HEAD_DIM = 128
GROUP = HEADS_Q // HEADS_KV
SCALE = 1.0 / math.sqrt(HEAD_DIM)
NEG_LARGE = -1e30
NT = (((1,), (1,)), ((), ()))
NN = (((1,), (0,)), ((), ()))
TN = (((0,), (0,)), ((), ()))


def dot(a, b, dims):
    return lax.dot_general(a, b, dims, preferred_element_type=jnp.float32)


def segment_facts(seq_ref, prompt_ref, positions):
    start = jnp.zeros_like(positions)
    first = jnp.zeros_like(positions)
    begin = 0
    for s in range(seq_ref.shape[0]):
        length = seq_ref[s]
        reached = positions >= begin
        start = jnp.where(reached, begin, start)
        first = jnp.where(reached, begin + jnp.minimum(prompt_ref[s], length - 1), first)
        begin = begin + length
    return start, first


def kernel(
    nctx, nhead, chunk,
    q_ref, k_ref, v_ref, og_ref, w_ref, seq_ref, prompt_ref,
    dq_ref, dk_ref, dv_ref,
    wbuf, ogbuf, acc, qs, gs, kbuf, vbuf, probs, peaks, top_ref, mass, dprobs, dqt, part, sib, total, sums, ret,
    w_sem, og_send, og_recv, k_send, v_send, k_recv, v_recv, k_fwd, v_fwd,
    sib_send, sib_recv, ret_send, ret_recv,
):
    count = q_ref.shape[0]
    kv_local = k_ref.shape[1] // HEAD_DIM
    chips = nctx // 4
    features = w_ref.shape[0]
    part_width = og_ref.shape[1]
    chunks = part_width // chunk
    me = lax.axis_index("ctx")
    head = lax.axis_index("head")
    half = me // (nctx // 2)
    base = half * (nctx // 2)
    core = me % 2
    other = 1 - core
    chip = (me - base) // 2
    sibling = me + 1 - 2 * core

    def remote(src, dst, send, recv, ctx, head_at):
        return pltpu.make_async_remote_copy(
            src_ref=src, dst_ref=dst, send_sem=send, recv_sem=recv,
            device_id=(ctx, head_at), device_id_type=pl.DeviceIdType.MESH,
        )

    def same_core(p):
        return base + 2 * p + core

    def w_copy(t):
        column = ((head + t // chunks) % nhead) * part_width + (t % chunks) * chunk
        return pltpu.make_async_copy(
            w_ref.at[:, pl.ds(pl.multiple_of(column, 128), chunk)], wbuf.at[t], w_sem.at[t]
        )

    for t in range(nhead * chunks):
        w_copy(t).start()

    barrier = pltpu.get_barrier_semaphore()

    def greet(ctx, head_at):
        pl.semaphore_signal(
            barrier, inc=1, device_id=(ctx, head_at), device_id_type=pl.DeviceIdType.MESH
        )

    for o in range(1, nhead):
        greet(me, (head + o) % nhead)
    greet(sibling, head)
    for o in range(1, chips):
        greet(same_core((chip + o) % chips), head)
    pl.semaphore_wait(barrier, nhead - 1 + 1 + chips - 1)

    def og_copy(o, ch):
        return remote(
            og_ref.at[:, pl.ds(ch * chunk, chunk)], ogbuf.at[o - 1, ch],
            og_send.at[o - 1, ch], og_recv.at[o - 1, ch], me, (head + nhead - o) % nhead,
        )

    for ch in range(chunks):
        for o in range(1, nhead):
            og_copy(o, ch).start()

    def direct(ref, buf, send, recv, p):
        return remote(ref, buf.at[chip, core], send.at[p], recv.at[chip, core], same_core(p), head)

    def to_sibling(ref, buf, send, recv, p):
        return remote(ref, buf.at[p, core], send.at[p], recv.at[p, core], sibling, head)

    def arrived(ref, buf, recv, p, c):
        pltpu.make_async_copy(ref, buf.at[p, c], recv.at[p, c]).wait()

    pairs = ((k_ref, kbuf, k_send, k_recv, k_fwd), (v_ref, vbuf, v_send, v_recv, v_fwd))
    def push(ref, buf, send, recv, fwd):
        to_sibling(ref, buf, fwd, recv, chip).start()

        def send_direct(p, carry):
            direct(ref, buf, send, recv, p).start()
            return carry

        lax.fori_loop(chip + 1, chips, send_direct, 0)
        buf[chip, core] = ref[...]

    push(*pairs[0])

    for c in range(kv_local):
        for g in range(GROUP):
            h = c * GROUP + g
            qs[c, g * count:(g + 1) * count, :] = q_ref[:, h * HEAD_DIM:(h + 1) * HEAD_DIM]

    tile = 640 if features % 640 == 0 else HEAD_DIM

    def project(rows, t, first):
        for n in range(0, features, tile):
            here = dot(rows, wbuf[t, n:n + tile, :], NT)
            if first:
                acc[:, n:n + tile] = here
            else:
                acc[:, n:n + tile] = acc[:, n:n + tile] + here

    key_rows = 2 * count
    columns = GROUP * count
    query_pos = me * count + lax.broadcasted_iota(jnp.int32, (1, count), 1)
    query_start, _ = segment_facts(seq_ref, prompt_ref, query_pos)
    mass[...] = jnp.zeros(mass.shape, jnp.float32)
    factor = SCALE * math.log2(math.e)

    def rows_of(buf, p, c):
        return buf[p, :, :, c * HEAD_DIM:(c + 1) * HEAD_DIM].reshape(key_rows, HEAD_DIM)

    def score_step(step):
        p = chip - step

        if not (isinstance(step, int) and step == 0):
            arrived(k_ref, kbuf, k_recv, p, core)
            to_sibling(kbuf.at[p, core], kbuf, k_fwd, k_recv, p).start()

        arrived(k_ref, kbuf, k_recv, p, other)
        key_pos = (base + 2 * p) * count + lax.broadcasted_iota(jnp.int32, (key_rows, count), 0)
        allowed = (key_pos <= query_pos) & (key_pos >= query_start)
        bias = jnp.where(allowed, 0.0, NEG_LARGE).astype(jnp.float32)
        bias = jnp.concatenate([bias] * GROUP, axis=1)
        for c in range(kv_local):
            scores = dot(rows_of(kbuf, p, c), qs[c], NT) + bias
            before = top_ref[c]
            top = jnp.maximum(before, jnp.max(scores, axis=0, keepdims=True))
            shrink = jnp.exp2((before - top) * factor)
            weights = jnp.exp2((scores - top) * factor)
            probs[c, p] = weights
            peaks[c, p] = top
            mass[c] = mass[c] * shrink + jnp.sum(weights, axis=0, keepdims=True)
            top_ref[c] = top

    top_ref[...] = jnp.full(top_ref.shape, 4.0 * NEG_LARGE, jnp.float32)
    score_step(0)
    push(*pairs[1])

    w_copy(0).wait()
    project(og_ref[:, :chunk], 0, True)

    def own_step(t, carry):
        w_copy(t).wait()
        project(og_ref[:, pl.ds(pl.multiple_of(t * chunk, chunk), chunk)], t, False)
        return carry

    lax.fori_loop(1, chunks, own_step, 0)

    def far_step(t, carry):
        o = t // chunks
        ch = t % chunks
        w_copy(t).wait()
        og_copy(o, ch).wait_recv()
        project(ogbuf[o - 1, ch], t, False)
        return carry

    far = (nhead - 1) * chunks - 1

    def mixed_step(step, carry):
        @pl.when(step <= chip)
        def _():
            score_step(step)

        lax.fori_loop(
            chunks + far * (step - 1) // (chips - 1), chunks + far * step // (chips - 1),
            far_step, 0,
        )
        return carry

    lax.fori_loop(1, chips, mixed_step, 0)

    for c in range(kv_local):
        inverse = 1.0 / mass[c]

        def scale_step(p, carry, c=c, inverse=inverse):
            peaks[c, p] = jnp.exp2((peaks[c, p] - top_ref[c]) * factor) * inverse
            return carry

        lax.fori_loop(0, chip + 1, scale_step, 0)
    def value_step(step, carry):
        p = chip - step
        arrived(v_ref, vbuf, v_recv, p, core)
        to_sibling(vbuf.at[p, core], vbuf, v_fwd, v_recv, p).start()
        return carry

    lax.fori_loop(1, chip + 1, value_step, 0)

    far_step(chunks + far, 0)

    row_pos = me * count + lax.broadcasted_iota(jnp.int32, (count, HEAD_DIM), 0)
    _, answer_first = segment_facts(seq_ref, prompt_ref, row_pos)
    answer = (row_pos >= answer_first).astype(jnp.float32)
    for c in range(kv_local):
        for g in range(GROUP):
            h = c * GROUP + g
            gs[c, g * count:(g + 1) * count, :] = (
                acc[:, h * HEAD_DIM:(h + 1) * HEAD_DIM] * answer
            ).astype(jnp.bfloat16)

    def sib_copy(c, p):
        return remote(
            part.at[c, p, other], sib.at[c, p], sib_send.at[c, p], sib_recv.at[c, p], sibling, head
        )

    def ret_copy(c, p):
        return remote(
            sums.at[c, p], ret.at[c, chip], ret_send.at[c, p], ret_recv.at[c, chip],
            same_core(p), head,
        )

    def combine(c, p):
        sib_copy(c, p).wait_recv()
        sums[c, p] = (
            part[c, p, core].astype(jnp.float32) + sib[c, p].astype(jnp.float32)
        ).astype(jnp.bfloat16)
        ret_copy(c, p).start()

    together = 2 if kv_local % 2 == 0 else 1
    for start in range(0, kv_local, together):
        heads = range(start, start + together)
        for c in heads:
            dqt[c - start] = jnp.zeros(dqt.shape[1:], jnp.float32)

        def delta_step(p, deltas, heads=heads, start=start):
            if start == 0:
                arrived(v_ref, vbuf, v_recv, p, other)
            found = []
            for c in heads:
                here = dot(rows_of(vbuf, p, c), gs[c], NT)
                dprobs[c - start, p] = here
                found.append(
                    deltas[c - start]
                    + jnp.sum(probs[c, p] * here, axis=0, keepdims=True) * peaks[c, p]
                )
            return tuple(found)

        deltas = lax.fori_loop(
            0, chip + 1, delta_step, (jnp.zeros((1, columns), jnp.float32),) * together
        )

        def grad_step(p, carry, heads=heads, deltas=deltas, start=start):
            for c in heads:
                weights = probs[c, p] * peaks[c, p]
                dvalue = dot(weights.astype(jnp.bfloat16), gs[c], NN)
                dscores = (weights * (dprobs[c - start, p] - deltas[c - start])).astype(jnp.bfloat16)
                dkey = dot(dscores, qs[c], NN) * SCALE
                dqt[c - start] = dqt[c - start] + dot(rows_of(kbuf, p, c), dscores, TN)
                part[c, p, :, 0] = dkey.astype(jnp.bfloat16).reshape(2, count, HEAD_DIM)
                part[c, p, :, 1] = dvalue.astype(jnp.bfloat16).reshape(2, count, HEAD_DIM)
                sib_copy(c, p).start()

            @pl.when(p > 0)
            def _():
                for c in heads:
                    combine(c, p - 1)

            return carry

        lax.fori_loop(0, chip + 1, grad_step, 0)
        for c in heads:
            for g in range(GROUP):
                h = c * GROUP + g
                dq_ref[:, h * HEAD_DIM:(h + 1) * HEAD_DIM] = (
                    dqt[c - start, :, g * count:(g + 1) * count].T * SCALE
                ).astype(jnp.bfloat16)

    for c in range(kv_local):
        sib_copy(c, chip).wait_recv()
        total[c] = part[c, chip, core].astype(jnp.float32) + sib[c, chip].astype(jnp.float32)

    for c in range(kv_local):
        def collect(p, carry, c=c):
            pltpu.make_async_copy(sums.at[c, 0], ret.at[c, p], ret_recv.at[c, p]).wait()
            total[c] = total[c] + ret[c, p].astype(jnp.float32)
            return carry

        lax.fori_loop(chip + 1, chips, collect, 0)
        dk_ref[:, c * HEAD_DIM:(c + 1) * HEAD_DIM] = total[c, 0].astype(jnp.bfloat16)
        dv_ref[:, c * HEAD_DIM:(c + 1) * HEAD_DIM] = total[c, 1].astype(jnp.bfloat16)

    for ch in range(chunks):
        for o in range(1, nhead):
            og_copy(o, ch).wait_send()
    for ref, buf, send, recv, fwd in pairs:
        def sent_direct(p, carry, ref=ref, buf=buf, send=send, recv=recv):
            direct(ref, buf, send, recv, p).wait_send()
            return carry

        lax.fori_loop(chip + 1, chips, sent_direct, 0)

        def sent_on(p, carry, ref=ref, buf=buf, fwd=fwd, recv=recv):
            to_sibling(ref, buf, fwd, recv, p).wait_send()
            return carry

        lax.fori_loop(0, chip + 1, sent_on, 0)
    for c in range(kv_local):
        def sent_part(p, carry, c=c):
            sib_copy(c, p).wait_send()
            return carry

        lax.fori_loop(0, chip + 1, sent_part, 0)

        def sent_sum(p, carry, c=c):
            ret_copy(c, p).wait_send()
            return carry

        lax.fori_loop(0, chip, sent_sum, 0)


def hand_on(*refs):
    sources, targets, held = refs[:3], refs[3:6], refs[6:9]
    sem = refs[9]
    loads = [pltpu.make_async_copy(sources[i], held[i], sem.at[i]) for i in range(3)]
    stores = [pltpu.make_async_copy(held[i], targets[i], sem.at[3 + i]) for i in range(3)]
    for load in loads:
        load.start()
    for load, store in zip(loads, stores):
        load.wait()
        store.start()
    for store in stores:
        store.wait()


def shards(queries, keys, values, out_grad, out_weight, seq_lengths, prompt_lengths):
    nctx = lax.axis_size("ctx")
    nhead = lax.axis_size("head")
    count = queries.shape[0]
    kv_local = keys.shape[1] // HEAD_DIM
    chips = nctx // 4
    features = out_weight.shape[0]
    width = out_grad.shape[1]
    chunk = 512 if width % 512 == 0 else 256
    chunks = width // chunk
    columns = GROUP * count
    bf16, f32 = jnp.bfloat16, jnp.float32
    vmem = pl.BlockSpec(memory_space=pltpu.VMEM)
    smem = pl.BlockSpec(memory_space=pltpu.SMEM)
    dma = pltpu.SemaphoreType.DMA
    far = max(nhead - 1, 1)
    results = pl.pallas_call(
        functools.partial(kernel, nctx, nhead, chunk),
        out_shape=(
            jax.ShapeDtypeStruct(queries.shape, bf16),
            jax.ShapeDtypeStruct(keys.shape, bf16),
            jax.ShapeDtypeStruct(values.shape, bf16),
        ),
        in_specs=[vmem, vmem, vmem, vmem, pl.BlockSpec(memory_space=pl.ANY), smem, smem],
        out_specs=(vmem, vmem, vmem),
        scratch_shapes=[
            pltpu.VMEM((nhead * chunks, features, chunk), bf16),
            pltpu.VMEM((far, chunks, count, chunk), bf16),
            pltpu.VMEM((count, features), f32),
            pltpu.VMEM((kv_local, columns, HEAD_DIM), bf16),
            pltpu.VMEM((kv_local, columns, HEAD_DIM), bf16),
            pltpu.VMEM((chips, 2, count, kv_local * HEAD_DIM), bf16),
            pltpu.VMEM((chips, 2, count, kv_local * HEAD_DIM), bf16),
            pltpu.VMEM((kv_local, chips, 2 * count, columns), f32),
            pltpu.VMEM((kv_local, chips, 1, columns), f32),
            pltpu.VMEM((kv_local, 1, columns), f32),
            pltpu.VMEM((kv_local, 1, columns), f32),
            pltpu.VMEM((2, chips, 2 * count, columns), f32),
            pltpu.VMEM((2, HEAD_DIM, columns), f32),
            pltpu.VMEM((kv_local, chips, 2, 2, count, HEAD_DIM), bf16),
            pltpu.VMEM((kv_local, chips, 2, count, HEAD_DIM), bf16),
            pltpu.VMEM((kv_local, 2, count, HEAD_DIM), f32),
            pltpu.VMEM((kv_local, chips, 2, count, HEAD_DIM), bf16),
            pltpu.VMEM((kv_local, chips, 2, count, HEAD_DIM), bf16),
            dma((nhead * chunks,)),
            dma((far, chunks)),
            dma((far, chunks)),
            dma((chips,)),
            dma((chips,)),
            dma((chips, 2)),
            dma((chips, 2)),
            dma((chips,)),
            dma((chips,)),
            dma((kv_local, chips)),
            dma((kv_local, chips)),
            dma((kv_local, chips)),
            dma((kv_local, chips)),
        ],
        compiler_params=pltpu.CompilerParams(
            collective_id=0, has_side_effects=True, vmem_limit_bytes=60 * 1024 * 1024
        ),
    )(queries, keys, values, out_grad, out_weight, seq_lengths, prompt_lengths)
    anywhere = pl.BlockSpec(memory_space=pl.ANY)
    return pl.pallas_call(
        hand_on,
        out_shape=tuple(jax.ShapeDtypeStruct(r.shape, r.dtype) for r in results),
        in_specs=[anywhere] * 3,
        out_specs=(anywhere,) * 3,
        scratch_shapes=[pltpu.VMEM(r.shape, r.dtype) for r in results] + [dma((6,))],
        compiler_params=pltpu.CompilerParams(vmem_limit_bytes=60 * 1024 * 1024),
    )(*results)


def solution(mesh):
    return jax.shard_map(
        shards,
        mesh=mesh,
        in_specs=(
            P("ctx", "head"),
            P("ctx", "head"),
            P("ctx", "head"),
            P("ctx", "head"),
            P("head", None),
            P(),
            P(),
        ),
        out_specs=(P("ctx", "head"), P("ctx", "head"), P("ctx", "head")),
        check_vma=False,
    )
```

```python
import functools
import math

import jax
import jax.numpy as jnp
from jax import lax
from jax.experimental import pallas as pl
from jax.experimental.pallas import tpu as pltpu
from jax.sharding import PartitionSpec as P

HEADS_Q = 40
HEADS_KV = 8
HEAD_DIM = 128
GROUP = HEADS_Q // HEADS_KV
SCALE = 1.0 / math.sqrt(HEAD_DIM)
NEG_LARGE = -1e30
NT = (((1,), (1,)), ((), ()))
NN = (((1,), (0,)), ((), ()))
TN = (((0,), (0,)), ((), ()))


def dot(a, b, dims):
    return lax.dot_general(a, b, dims, preferred_element_type=jnp.float32)


def segment_facts(seq_ref, prompt_ref, positions):
    start = jnp.zeros_like(positions)
    first = jnp.zeros_like(positions)
    begin = 0
    for s in range(seq_ref.shape[0]):
        length = seq_ref[s]
        reached = positions >= begin
        start = jnp.where(reached, begin, start)
        first = jnp.where(reached, begin + jnp.minimum(prompt_ref[s], length - 1), first)
        begin = begin + length
    return start, first


def kernel(
    nctx, nhead, chunk,
    q_ref, k_ref, v_ref, og_ref, w_ref, seq_ref, prompt_ref,
    dq_ref, dk_ref, dv_ref,
    ogown, dqv, wbuf, ogbuf, acc, qs, gs, kbuf, vbuf, probs, peaks, top_ref, mass, dprobs, dqt, part, sib, total, sums, ret,
    og_sem, q_sem, dq_sem, w_sem, og_send, og_recv, k_send, v_send, k_recv, v_recv, k_fwd, v_fwd,
    sib_send, sib_recv, ret_send, ret_recv,
):
    count = q_ref.shape[0]
    kv_local = k_ref.shape[1] // HEAD_DIM
    chips = nctx // 4
    features = w_ref.shape[0]
    part_width = og_ref.shape[1]
    chunks = part_width // chunk
    me = lax.axis_index("ctx")
    head = lax.axis_index("head")
    half = me // (nctx // 2)
    base = half * (nctx // 2)
    core = me % 2
    other = 1 - core
    chip = (me - base) // 2
    sibling = me + 1 - 2 * core

    def remote(src, dst, send, recv, ctx, head_at):
        return pltpu.make_async_remote_copy(
            src_ref=src, dst_ref=dst, send_sem=send, recv_sem=recv,
            device_id=(ctx, head_at), device_id_type=pl.DeviceIdType.MESH,
        )

    def same_core(p):
        return base + 2 * p + core

    def w_copy(t):
        column = ((head + t // chunks) % nhead) * part_width + (t % chunks) * chunk
        return pltpu.make_async_copy(
            w_ref.at[:, pl.ds(pl.multiple_of(column, 128), chunk)], wbuf.at[t], w_sem.at[t]
        )

    og_local = pltpu.make_async_copy(og_ref, ogown, og_sem)
    k_local = pltpu.make_async_copy(k_ref, kbuf.at[chip, core], k_recv.at[chip, core])
    v_local = pltpu.make_async_copy(v_ref, vbuf.at[chip, core], v_recv.at[chip, core])

    def q_copy(c, g):
        h = c * GROUP + g
        return pltpu.make_async_copy(
            q_ref.at[:, pl.ds(h * HEAD_DIM, HEAD_DIM)],
            qs.at[c, pl.ds(g * count, count)], q_sem.at[c, g],
        )

    all_heads = [(c, g) for c in range(kv_local) for g in range(GROUP)]
    k_local.start()
    for c, g in all_heads:
        q_copy(c, g).start()
    og_local.start()
    v_local.start()
    early = 2
    for t in range(early):
        w_copy(t).start()

    barrier = pltpu.get_barrier_semaphore()

    def greet(ctx, head_at):
        pl.semaphore_signal(
            barrier, inc=1, device_id=(ctx, head_at), device_id_type=pl.DeviceIdType.MESH
        )

    for o in range(1, nhead):
        greet(me, (head + o) % nhead)
    greet(sibling, head)
    for o in range(1, chips):
        greet(same_core((chip + o) % chips), head)
    pl.semaphore_wait(barrier, nhead - 1 + 1 + chips - 1)

    def og_copy(o, ch):
        return remote(
            og_ref.at[:, pl.ds(ch * chunk, chunk)], ogbuf.at[o - 1, ch],
            og_send.at[o - 1, ch], og_recv.at[o - 1, ch], me, (head + nhead - o) % nhead,
        )

    for ch in range(chunks):
        for o in range(1, nhead):
            og_copy(o, ch).start()

    def direct(ref, buf, send, recv, p):
        return remote(ref, buf.at[chip, core], send.at[p], recv.at[chip, core], same_core(p), head)

    def to_sibling(ref, buf, send, recv, p):
        return remote(ref, buf.at[p, core], send.at[p], recv.at[p, core], sibling, head)

    def arrived(ref, buf, recv, p, c):
        pltpu.make_async_copy(ref, buf.at[p, c], recv.at[p, c]).wait()

    pairs = ((k_ref, kbuf, k_send, k_recv, k_fwd), (v_ref, vbuf, v_send, v_recv, v_fwd))
    def push(ref, buf, send, recv, fwd):
        to_sibling(ref, buf, fwd, recv, chip).start()

        def send_direct(p, carry):
            direct(ref, buf, send, recv, p).start()
            return carry

        lax.fori_loop(chip + 1, chips, send_direct, 0)

    push(*pairs[0])
    for t in range(early, nhead * chunks):
        w_copy(t).start()
    for c, g in all_heads:
        q_copy(c, g).wait()
    k_local.wait()

    tile = 640 if features % 640 == 0 else HEAD_DIM

    def project(rows, t, first):
        for n in range(0, features, tile):
            here = dot(rows, wbuf[t, n:n + tile, :], NT)
            if first:
                acc[:, n:n + tile] = here
            else:
                acc[:, n:n + tile] = acc[:, n:n + tile] + here

    key_rows = 2 * count
    columns = GROUP * count
    query_pos = me * count + lax.broadcasted_iota(jnp.int32, (1, count), 1)
    query_start, _ = segment_facts(seq_ref, prompt_ref, query_pos)
    mass[...] = jnp.zeros(mass.shape, jnp.float32)
    factor = SCALE * math.log2(math.e)

    def rows_of(buf, p, c):
        return buf[p, :, :, c * HEAD_DIM:(c + 1) * HEAD_DIM].reshape(key_rows, HEAD_DIM)

    def score_step(step):
        p = chip - step

        if not (isinstance(step, int) and step == 0):
            arrived(k_ref, kbuf, k_recv, p, core)
            to_sibling(kbuf.at[p, core], kbuf, k_fwd, k_recv, p).start()

        arrived(k_ref, kbuf, k_recv, p, other)
        key_pos = (base + 2 * p) * count + lax.broadcasted_iota(jnp.int32, (key_rows, count), 0)
        allowed = (key_pos <= query_pos) & (key_pos >= query_start)
        bias = jnp.where(allowed, 0.0, NEG_LARGE).astype(jnp.float32)
        bias = jnp.concatenate([bias] * GROUP, axis=1)
        for c in range(kv_local):
            scores = dot(rows_of(kbuf, p, c), qs[c], NT) + bias
            before = top_ref[c]
            top = jnp.maximum(before, jnp.max(scores, axis=0, keepdims=True))
            shrink = jnp.exp2((before - top) * factor)
            weights = jnp.exp2((scores - top) * factor)
            probs[c, p] = weights
            peaks[c, p] = top
            mass[c] = mass[c] * shrink + jnp.sum(weights, axis=0, keepdims=True)
            top_ref[c] = top

    top_ref[...] = jnp.full(top_ref.shape, 4.0 * NEG_LARGE, jnp.float32)
    score_step(0)
    push(*pairs[1])

    w_copy(0).wait()
    og_local.wait()
    project(ogown[:, :chunk], 0, True)

    def own_step(t, carry):
        w_copy(t).wait()
        project(ogown[:, pl.ds(pl.multiple_of(t * chunk, chunk), chunk)], t, False)
        return carry

    lax.fori_loop(1, chunks, own_step, 0)

    def far_step(t, carry):
        o = t // chunks
        ch = t % chunks
        w_copy(t).wait()
        og_copy(o, ch).wait_recv()
        project(ogbuf[o - 1, ch], t, False)
        return carry

    far = (nhead - 1) * chunks - 1

    def mixed_step(step, carry):
        @pl.when(step <= chip)
        def _():
            score_step(step)

        lax.fori_loop(
            chunks + far * (step - 1) // (chips - 1), chunks + far * step // (chips - 1),
            far_step, 0,
        )
        return carry

    lax.fori_loop(1, chips, mixed_step, 0)

    for c in range(kv_local):
        inverse = 1.0 / mass[c]

        def scale_step(p, carry, c=c, inverse=inverse):
            peaks[c, p] = jnp.exp2((peaks[c, p] - top_ref[c]) * factor) * inverse
            return carry

        lax.fori_loop(0, chip + 1, scale_step, 0)
    v_local.wait()

    def value_step(step, carry):
        p = chip - step
        arrived(v_ref, vbuf, v_recv, p, core)
        to_sibling(vbuf.at[p, core], vbuf, v_fwd, v_recv, p).start()
        return carry

    lax.fori_loop(1, chip + 1, value_step, 0)

    far_step(chunks + far, 0)

    row_pos = me * count + lax.broadcasted_iota(jnp.int32, (count, HEAD_DIM), 0)
    _, answer_first = segment_facts(seq_ref, prompt_ref, row_pos)
    answer = (row_pos >= answer_first).astype(jnp.float32)
    for c in range(kv_local):
        for g in range(GROUP):
            h = c * GROUP + g
            gs[c, g * count:(g + 1) * count, :] = (
                acc[:, h * HEAD_DIM:(h + 1) * HEAD_DIM] * answer
            ).astype(jnp.bfloat16)

    def sib_copy(c, p):
        return remote(
            part.at[c, p, other], sib.at[c, p], sib_send.at[c, p], sib_recv.at[c, p], sibling, head
        )

    def ret_copy(c, p):
        return remote(
            sums.at[c, p], ret.at[c, chip], ret_send.at[c, p], ret_recv.at[c, chip],
            same_core(p), head,
        )

    def combine(c, p):
        sib_copy(c, p).wait_recv()
        sums[c, p] = (
            part[c, p, core].astype(jnp.float32) + sib[c, p].astype(jnp.float32)
        ).astype(jnp.bfloat16)
        ret_copy(c, p).start()

    def dq_copy(start):
        lanes = pl.ds(start * GROUP * HEAD_DIM, together * GROUP * HEAD_DIM)
        return pltpu.make_async_copy(
            dqv.at[:, lanes], dq_ref.at[:, lanes], dq_sem.at[start // together]
        )

    together = 2 if kv_local % 2 == 0 else 1
    for start in range(0, kv_local, together):
        heads = range(start, start + together)
        for c in heads:
            dqt[c - start] = jnp.zeros(dqt.shape[1:], jnp.float32)

        def delta_step(p, deltas, heads=heads, start=start):
            if start == 0:
                arrived(v_ref, vbuf, v_recv, p, other)
            found = []
            for c in heads:
                here = dot(rows_of(vbuf, p, c), gs[c], NT)
                dprobs[c - start, p] = here
                found.append(
                    deltas[c - start]
                    + jnp.sum(probs[c, p] * here, axis=0, keepdims=True) * peaks[c, p]
                )
            return tuple(found)

        deltas = lax.fori_loop(
            0, chip + 1, delta_step, (jnp.zeros((1, columns), jnp.float32),) * together
        )

        def grad_step(p, carry, heads=heads, deltas=deltas, start=start):
            for c in heads:
                weights = probs[c, p] * peaks[c, p]
                dvalue = dot(weights.astype(jnp.bfloat16), gs[c], NN)
                dscores = (weights * (dprobs[c - start, p] - deltas[c - start])).astype(jnp.bfloat16)
                dkey = dot(dscores, qs[c], NN) * SCALE
                dqt[c - start] = dqt[c - start] + dot(rows_of(kbuf, p, c), dscores, TN)
                part[c, p, :, 0] = dkey.astype(jnp.bfloat16).reshape(2, count, HEAD_DIM)
                part[c, p, :, 1] = dvalue.astype(jnp.bfloat16).reshape(2, count, HEAD_DIM)
                sib_copy(c, p).start()

            @pl.when(p > 0)
            def _():
                for c in heads:
                    combine(c, p - 1)

            return carry

        lax.fori_loop(0, chip + 1, grad_step, 0)
        for c in heads:
            for g in range(GROUP):
                h = c * GROUP + g
                dqv[:, h * HEAD_DIM:(h + 1) * HEAD_DIM] = (
                    dqt[c - start, :, g * count:(g + 1) * count].T * SCALE
                ).astype(jnp.bfloat16)
        dq_copy(start).start()

    for c in range(kv_local):
        sib_copy(c, chip).wait_recv()
        total[c] = part[c, chip, core].astype(jnp.float32) + sib[c, chip].astype(jnp.float32)

    for c in range(kv_local):
        def collect(p, carry, c=c):
            pltpu.make_async_copy(sums.at[c, 0], ret.at[c, p], ret_recv.at[c, p]).wait()
            total[c] = total[c] + ret[c, p].astype(jnp.float32)
            return carry

        lax.fori_loop(chip + 1, chips, collect, 0)
        dk_ref[:, c * HEAD_DIM:(c + 1) * HEAD_DIM] = total[c, 0].astype(jnp.bfloat16)
        dv_ref[:, c * HEAD_DIM:(c + 1) * HEAD_DIM] = total[c, 1].astype(jnp.bfloat16)

    for start in range(0, kv_local, together):
        dq_copy(start).wait()
    for ch in range(chunks):
        for o in range(1, nhead):
            og_copy(o, ch).wait_send()
    for ref, buf, send, recv, fwd in pairs:
        def sent_direct(p, carry, ref=ref, buf=buf, send=send, recv=recv):
            direct(ref, buf, send, recv, p).wait_send()
            return carry

        lax.fori_loop(chip + 1, chips, sent_direct, 0)

        def sent_on(p, carry, ref=ref, buf=buf, fwd=fwd, recv=recv):
            to_sibling(ref, buf, fwd, recv, p).wait_send()
            return carry

        lax.fori_loop(0, chip + 1, sent_on, 0)
    for c in range(kv_local):
        def sent_part(p, carry, c=c):
            sib_copy(c, p).wait_send()
            return carry

        lax.fori_loop(0, chip + 1, sent_part, 0)

        def sent_sum(p, carry, c=c):
            ret_copy(c, p).wait_send()
            return carry

        lax.fori_loop(0, chip, sent_sum, 0)


def hand_on(*refs):
    sources, targets, held = refs[:3], refs[3:6], refs[6:9]
    sem = refs[9]
    loads = [pltpu.make_async_copy(sources[i], held[i], sem.at[i]) for i in range(3)]
    stores = [pltpu.make_async_copy(held[i], targets[i], sem.at[3 + i]) for i in range(3)]
    for load in loads:
        load.start()
    for load, store in zip(loads, stores):
        load.wait()
        store.start()
    for store in stores:
        store.wait()


def shards(queries, keys, values, out_grad, out_weight, seq_lengths, prompt_lengths):
    nctx = lax.axis_size("ctx")
    nhead = lax.axis_size("head")
    count = queries.shape[0]
    kv_local = keys.shape[1] // HEAD_DIM
    chips = nctx // 4
    features = out_weight.shape[0]
    width = out_grad.shape[1]
    chunk = 512 if width % 512 == 0 else 256
    chunks = width // chunk
    columns = GROUP * count
    bf16, f32 = jnp.bfloat16, jnp.float32
    vmem = pl.BlockSpec(memory_space=pltpu.VMEM)
    smem = pl.BlockSpec(memory_space=pltpu.SMEM)
    dma = pltpu.SemaphoreType.DMA
    far = max(nhead - 1, 1)
    results = pl.pallas_call(
        functools.partial(kernel, nctx, nhead, chunk),
        out_shape=(
            jax.ShapeDtypeStruct(queries.shape, bf16),
            jax.ShapeDtypeStruct(keys.shape, bf16),
            jax.ShapeDtypeStruct(values.shape, bf16),
        ),
        in_specs=[pl.BlockSpec(memory_space=pl.ANY)] * 5 + [smem, smem],
        out_specs=(pl.BlockSpec(memory_space=pl.ANY), vmem, vmem),
        scratch_shapes=[
            pltpu.VMEM(out_grad.shape, bf16),
            pltpu.VMEM(queries.shape, bf16),
            pltpu.VMEM((nhead * chunks, features, chunk), bf16),
            pltpu.VMEM((far, chunks, count, chunk), bf16),
            pltpu.VMEM((count, features), f32),
            pltpu.VMEM((kv_local, columns, HEAD_DIM), bf16),
            pltpu.VMEM((kv_local, columns, HEAD_DIM), bf16),
            pltpu.VMEM((chips, 2, count, kv_local * HEAD_DIM), bf16),
            pltpu.VMEM((chips, 2, count, kv_local * HEAD_DIM), bf16),
            pltpu.VMEM((kv_local, chips, 2 * count, columns), f32),
            pltpu.VMEM((kv_local, chips, 1, columns), f32),
            pltpu.VMEM((kv_local, 1, columns), f32),
            pltpu.VMEM((kv_local, 1, columns), f32),
            pltpu.VMEM((2, chips, 2 * count, columns), f32),
            pltpu.VMEM((2, HEAD_DIM, columns), f32),
            pltpu.VMEM((kv_local, chips, 2, 2, count, HEAD_DIM), bf16),
            pltpu.VMEM((kv_local, chips, 2, count, HEAD_DIM), bf16),
            pltpu.VMEM((kv_local, 2, count, HEAD_DIM), f32),
            pltpu.VMEM((kv_local, chips, 2, count, HEAD_DIM), bf16),
            pltpu.VMEM((kv_local, chips, 2, count, HEAD_DIM), bf16),
            dma(()),
            dma((kv_local, GROUP)),
            dma((kv_local,)),
            dma((nhead * chunks,)),
            dma((far, chunks)),
            dma((far, chunks)),
            dma((chips,)),
            dma((chips,)),
            dma((chips, 2)),
            dma((chips, 2)),
            dma((chips,)),
            dma((chips,)),
            dma((kv_local, chips)),
            dma((kv_local, chips)),
            dma((kv_local, chips)),
            dma((kv_local, chips)),
        ],
        compiler_params=pltpu.CompilerParams(
            collective_id=0, has_side_effects=True, vmem_limit_bytes=60 * 1024 * 1024
        ),
    )(queries, keys, values, out_grad, out_weight, seq_lengths, prompt_lengths)
    anywhere = pl.BlockSpec(memory_space=pl.ANY)
    return pl.pallas_call(
        hand_on,
        out_shape=tuple(jax.ShapeDtypeStruct(r.shape, r.dtype) for r in results),
        in_specs=[anywhere] * 3,
        out_specs=(anywhere,) * 3,
        scratch_shapes=[pltpu.VMEM(r.shape, r.dtype) for r in results] + [dma((6,))],
        compiler_params=pltpu.CompilerParams(vmem_limit_bytes=60 * 1024 * 1024),
    )(*results)


def solution(mesh):
    return jax.shard_map(
        shards,
        mesh=mesh,
        in_specs=(
            P("ctx", "head"),
            P("ctx", "head"),
            P("ctx", "head"),
            P("ctx", "head"),
            P("head", None),
            P(),
            P(),
        ),
        out_specs=(P("ctx", "head"), P("ctx", "head"), P("ctx", "head")),
        check_vma=False,
    )
```

```python
import functools
import math

import jax
import jax.numpy as jnp
from jax import lax
from jax.experimental import pallas as pl
from jax.experimental.pallas import tpu as pltpu
from jax.sharding import PartitionSpec as P

HEADS_Q = 40
HEADS_KV = 8
HEAD_DIM = 128
GROUP = HEADS_Q // HEADS_KV
SCALE = 1.0 / math.sqrt(HEAD_DIM)
NEG_LARGE = -1e30
NT = (((1,), (1,)), ((), ()))
NN = (((1,), (0,)), ((), ()))
TN = (((0,), (0,)), ((), ()))


def dot(a, b, dims):
    return lax.dot_general(a, b, dims, preferred_element_type=jnp.float32)


def segment_facts(seq_ref, prompt_ref, positions):
    start = jnp.zeros_like(positions)
    first = jnp.zeros_like(positions)
    begin = 0
    for s in range(seq_ref.shape[0]):
        length = seq_ref[s]
        reached = positions >= begin
        start = jnp.where(reached, begin, start)
        first = jnp.where(reached, begin + jnp.minimum(prompt_ref[s], length - 1), first)
        begin = begin + length
    return start, first


def kernel(
    nctx, nhead, chunk,
    q_ref, k_ref, v_ref, og_ref, w_ref, seq_ref, prompt_ref,
    dq_ref, dk_ref, dv_ref,
    ogown, dqv, wbuf, ogbuf, acc, qs, gs, kbuf, vbuf, probs, peaks, top_ref, mass, dprobs, dqt, part, sib, total, sums, ret,
    og_sem, q_sem, dq_sem, w_sem, og_send, og_recv, k_send, v_send, k_recv, v_recv, k_fwd, v_fwd,
    sib_send, sib_recv, ret_send, ret_recv,
):
    count = q_ref.shape[0]
    kv_local = k_ref.shape[1] // HEAD_DIM
    chips = nctx // 4
    features = w_ref.shape[0]
    part_width = og_ref.shape[1]
    chunks = part_width // chunk
    me = lax.axis_index("ctx")
    head = lax.axis_index("head")
    half = me // (nctx // 2)
    base = half * (nctx // 2)
    core = me % 2
    other = 1 - core
    chip = (me - base) // 2
    sibling = me + 1 - 2 * core

    def remote(src, dst, send, recv, ctx, head_at):
        return pltpu.make_async_remote_copy(
            src_ref=src, dst_ref=dst, send_sem=send, recv_sem=recv,
            device_id=(ctx, head_at), device_id_type=pl.DeviceIdType.MESH,
        )

    def same_core(p):
        return base + 2 * p + core

    def w_copy(t):
        column = ((head + t // chunks) % nhead) * part_width + (t % chunks) * chunk
        return pltpu.make_async_copy(
            w_ref.at[:, pl.ds(pl.multiple_of(column, 128), chunk)], wbuf.at[t], w_sem.at[t]
        )

    og_local = pltpu.make_async_copy(og_ref, ogown, og_sem)
    k_local = pltpu.make_async_copy(k_ref, kbuf.at[chip, core], k_recv.at[chip, core])
    v_local = pltpu.make_async_copy(v_ref, vbuf.at[chip, core], v_recv.at[chip, core])

    def q_copy(c, g):
        h = c * GROUP + g
        return pltpu.make_async_copy(
            q_ref.at[:, pl.ds(h * HEAD_DIM, HEAD_DIM)],
            qs.at[c, pl.ds(g * count, count)], q_sem.at[c, g],
        )

    all_heads = [(c, g) for c in range(kv_local) for g in range(GROUP)]
    k_local.start()
    for c, g in all_heads:
        q_copy(c, g).start()
    og_local.start()
    v_local.start()
    early = 2
    for t in range(early):
        w_copy(t).start()

    barrier = pltpu.get_barrier_semaphore()

    def greet(ctx, head_at):
        pl.semaphore_signal(
            barrier, inc=1, device_id=(ctx, head_at), device_id_type=pl.DeviceIdType.MESH
        )

    for o in range(1, nhead):
        greet(me, (head + o) % nhead)
    greet(sibling, head)
    for o in range(1, chips):
        greet(same_core((chip + o) % chips), head)
    pl.semaphore_wait(barrier, nhead - 1 + 1 + chips - 1)

    def og_copy(o, ch):
        return remote(
            og_ref.at[:, pl.ds(ch * chunk, chunk)], ogbuf.at[o - 1, ch],
            og_send.at[o - 1, ch], og_recv.at[o - 1, ch], me, (head + nhead - o) % nhead,
        )

    for ch in range(chunks):
        for o in range(1, nhead):
            og_copy(o, ch).start()

    def direct(ref, buf, send, recv, p):
        return remote(ref, buf.at[chip, core], send.at[p], recv.at[chip, core], same_core(p), head)

    def to_sibling(ref, buf, send, recv, p):
        return remote(ref, buf.at[p, core], send.at[p], recv.at[p, core], sibling, head)

    def arrived(ref, buf, recv, p, c):
        pltpu.make_async_copy(ref, buf.at[p, c], recv.at[p, c]).wait()

    pairs = ((k_ref, kbuf, k_send, k_recv, k_fwd), (v_ref, vbuf, v_send, v_recv, v_fwd))
    def push(ref, buf, send, recv, fwd):
        to_sibling(ref, buf, fwd, recv, chip).start()

        def send_direct(p, carry):
            direct(ref, buf, send, recv, p).start()
            return carry

        lax.fori_loop(chip + 1, chips, send_direct, 0)

    push(*pairs[0])
    for t in range(early, nhead * chunks):
        w_copy(t).start()
    for c, g in all_heads:
        q_copy(c, g).wait()
    k_local.wait()

    tile = 640 if features % 640 == 0 else HEAD_DIM

    def project(rows, t, first):
        for n in range(0, features, tile):
            here = dot(rows, wbuf[t, n:n + tile, :], NT)
            if first:
                acc[:, n:n + tile] = here
            else:
                acc[:, n:n + tile] = acc[:, n:n + tile] + here

    key_rows = 2 * count
    columns = GROUP * count
    query_pos = me * count + lax.broadcasted_iota(jnp.int32, (1, count), 1)
    query_start, _ = segment_facts(seq_ref, prompt_ref, query_pos)
    mass[...] = jnp.zeros(mass.shape, jnp.float32)
    factor = SCALE * math.log2(math.e)

    def rows_of(buf, p, c):
        return buf[p, :, :, c * HEAD_DIM:(c + 1) * HEAD_DIM].reshape(key_rows, HEAD_DIM)

    def score_step(step):
        p = chip - step

        if not (isinstance(step, int) and step == 0):
            arrived(k_ref, kbuf, k_recv, p, core)
            to_sibling(kbuf.at[p, core], kbuf, k_fwd, k_recv, p).start()

        arrived(k_ref, kbuf, k_recv, p, other)
        key_pos = (base + 2 * p) * count + lax.broadcasted_iota(jnp.int32, (key_rows, count), 0)
        allowed = (key_pos <= query_pos) & (key_pos >= query_start)
        bias = jnp.where(allowed, 0.0, NEG_LARGE).astype(jnp.float32)
        bias = jnp.concatenate([bias] * GROUP, axis=1)
        for c in range(kv_local):
            scores = dot(rows_of(kbuf, p, c), qs[c], NT) + bias
            before = top_ref[c]
            top = jnp.maximum(before, jnp.max(scores, axis=0, keepdims=True))
            shrink = jnp.exp2((before - top) * factor)
            weights = jnp.exp2((scores - top) * factor)
            probs[c, p] = weights
            peaks[c, p] = top
            mass[c] = mass[c] * shrink + jnp.sum(weights, axis=0, keepdims=True)
            top_ref[c] = top

    top_ref[...] = jnp.full(top_ref.shape, 4.0 * NEG_LARGE, jnp.float32)
    score_step(0)
    push(*pairs[1])

    w_copy(0).wait()
    og_local.wait()
    project(ogown[:, :chunk], 0, True)

    def own_step(t, carry):
        w_copy(t).wait()
        project(ogown[:, pl.ds(pl.multiple_of(t * chunk, chunk), chunk)], t, False)
        return carry

    lax.fori_loop(1, chunks, own_step, 0)

    def far_step(t, carry):
        o = t // chunks
        ch = t % chunks
        w_copy(t).wait()
        og_copy(o, ch).wait_recv()
        project(ogbuf[o - 1, ch], t, False)
        return carry

    far = (nhead - 1) * chunks - 1

    def mixed_step(step, carry):
        @pl.when(step <= chip)
        def _():
            score_step(step)

        lax.fori_loop(
            chunks + far * (step - 1) // (chips - 1), chunks + far * step // (chips - 1),
            far_step, 0,
        )
        return carry

    lax.fori_loop(1, chips, mixed_step, 0)

    for c in range(kv_local):
        inverse = 1.0 / mass[c]

        def scale_step(p, carry, c=c, inverse=inverse):
            peaks[c, p] = jnp.exp2((peaks[c, p] - top_ref[c]) * factor) * inverse
            return carry

        lax.fori_loop(0, chip + 1, scale_step, 0)
    v_local.wait()

    def value_step(step, carry):
        p = chip - step
        arrived(v_ref, vbuf, v_recv, p, core)
        to_sibling(vbuf.at[p, core], vbuf, v_fwd, v_recv, p).start()
        return carry

    lax.fori_loop(1, chip + 1, value_step, 0)

    far_step(chunks + far, 0)

    row_pos = me * count + lax.broadcasted_iota(jnp.int32, (count, HEAD_DIM), 0)
    _, answer_first = segment_facts(seq_ref, prompt_ref, row_pos)
    answer = (row_pos >= answer_first).astype(jnp.float32)
    for c in range(kv_local):
        for g in range(GROUP):
            h = c * GROUP + g
            gs[c, g * count:(g + 1) * count, :] = (
                acc[:, h * HEAD_DIM:(h + 1) * HEAD_DIM] * answer
            ).astype(jnp.bfloat16)

    def sib_copy(c, p):
        return remote(
            part.at[c, p, other], sib.at[c, p], sib_send.at[c, p], sib_recv.at[c, p], sibling, head
        )

    def ret_copy(c, p):
        return remote(
            sums.at[c, p], ret.at[c, chip], ret_send.at[c, p], ret_recv.at[c, chip],
            same_core(p), head,
        )

    def combine(c, p):
        sib_copy(c, p).wait_recv()
        sums[c, p] = (
            part[c, p, core].astype(jnp.float32) + sib[c, p].astype(jnp.float32)
        ).astype(jnp.bfloat16)
        ret_copy(c, p).start()

    def dq_copy(start):
        lanes = pl.ds(start * GROUP * HEAD_DIM, together * GROUP * HEAD_DIM)
        return pltpu.make_async_copy(
            dqv.at[:, lanes], dq_ref.at[:, lanes], dq_sem.at[start // together]
        )

    together = 2 if kv_local % 2 == 0 else 1
    for start in range(0, kv_local, together):
        heads = range(start, start + together)
        for c in heads:
            dqt[c - start] = jnp.zeros(dqt.shape[1:], jnp.float32)

        def delta_step(p, deltas, heads=heads, start=start):
            if start == 0:
                arrived(v_ref, vbuf, v_recv, p, other)
            found = []
            for c in heads:
                here = dot(rows_of(vbuf, p, c), gs[c], NT)
                dprobs[c - start, p] = here
                found.append(
                    deltas[c - start]
                    + jnp.sum(probs[c, p] * here, axis=0, keepdims=True) * peaks[c, p]
                )
            return tuple(found)

        deltas = lax.fori_loop(
            0, chip + 1, delta_step, (jnp.zeros((1, columns), jnp.float32),) * together
        )

        def grad_step(p, carry, heads=heads, deltas=deltas, start=start):
            for c in heads:
                weights = probs[c, p] * peaks[c, p]
                dvalue = dot(weights.astype(jnp.bfloat16), gs[c], NN)
                dscores = (weights * (dprobs[c - start, p] - deltas[c - start])).astype(jnp.bfloat16)
                dkey = dot(dscores, qs[c], NN) * SCALE
                dqt[c - start] = dqt[c - start] + dot(rows_of(kbuf, p, c), dscores, TN)
                part[c, p, :, 0] = dkey.astype(jnp.bfloat16).reshape(2, count, HEAD_DIM)
                part[c, p, :, 1] = dvalue.astype(jnp.bfloat16).reshape(2, count, HEAD_DIM)
                sib_copy(c, p).start()
                if c == start:
                    @pl.when(p > 0)
                    def _():
                        for earlier in heads:
                            combine(earlier, p - 1)


            return carry

        lax.fori_loop(0, chip + 1, grad_step, 0)
        for c in heads:
            for g in range(GROUP):
                h = c * GROUP + g
                dqv[:, h * HEAD_DIM:(h + 1) * HEAD_DIM] = (
                    dqt[c - start, :, g * count:(g + 1) * count].T * SCALE
                ).astype(jnp.bfloat16)
        dq_copy(start).start()

    for c in range(kv_local):
        sib_copy(c, chip).wait_recv()
        total[c] = part[c, chip, core].astype(jnp.float32) + sib[c, chip].astype(jnp.float32)

    for c in range(kv_local):
        def collect(p, carry, c=c):
            pltpu.make_async_copy(sums.at[c, 0], ret.at[c, p], ret_recv.at[c, p]).wait()
            total[c] = total[c] + ret[c, p].astype(jnp.float32)
            return carry

        lax.fori_loop(chip + 1, chips, collect, 0)
        dk_ref[:, c * HEAD_DIM:(c + 1) * HEAD_DIM] = total[c, 0].astype(jnp.bfloat16)
        dv_ref[:, c * HEAD_DIM:(c + 1) * HEAD_DIM] = total[c, 1].astype(jnp.bfloat16)

    for start in range(0, kv_local, together):
        dq_copy(start).wait()
    for ch in range(chunks):
        for o in range(1, nhead):
            og_copy(o, ch).wait_send()
    for ref, buf, send, recv, fwd in pairs:
        def sent_direct(p, carry, ref=ref, buf=buf, send=send, recv=recv):
            direct(ref, buf, send, recv, p).wait_send()
            return carry

        lax.fori_loop(chip + 1, chips, sent_direct, 0)

        def sent_on(p, carry, ref=ref, buf=buf, fwd=fwd, recv=recv):
            to_sibling(ref, buf, fwd, recv, p).wait_send()
            return carry

        lax.fori_loop(0, chip + 1, sent_on, 0)
    for c in range(kv_local):
        def sent_part(p, carry, c=c):
            sib_copy(c, p).wait_send()
            return carry

        lax.fori_loop(0, chip + 1, sent_part, 0)

        def sent_sum(p, carry, c=c):
            ret_copy(c, p).wait_send()
            return carry

        lax.fori_loop(0, chip, sent_sum, 0)


def hand_on(*refs):
    sources, targets, held = refs[:3], refs[3:6], refs[6:9]
    sem = refs[9]
    loads = [pltpu.make_async_copy(sources[i], held[i], sem.at[i]) for i in range(3)]
    stores = [pltpu.make_async_copy(held[i], targets[i], sem.at[3 + i]) for i in range(3)]
    for load in loads:
        load.start()
    for load, store in zip(loads, stores):
        load.wait()
        store.start()
    for store in stores:
        store.wait()


def shards(queries, keys, values, out_grad, out_weight, seq_lengths, prompt_lengths):
    nctx = lax.axis_size("ctx")
    nhead = lax.axis_size("head")
    count = queries.shape[0]
    kv_local = keys.shape[1] // HEAD_DIM
    chips = nctx // 4
    features = out_weight.shape[0]
    width = out_grad.shape[1]
    chunk = 512 if width % 512 == 0 else 256
    chunks = width // chunk
    columns = GROUP * count
    bf16, f32 = jnp.bfloat16, jnp.float32
    vmem = pl.BlockSpec(memory_space=pltpu.VMEM)
    smem = pl.BlockSpec(memory_space=pltpu.SMEM)
    dma = pltpu.SemaphoreType.DMA
    far = max(nhead - 1, 1)
    results = pl.pallas_call(
        functools.partial(kernel, nctx, nhead, chunk),
        out_shape=(
            jax.ShapeDtypeStruct(queries.shape, bf16),
            jax.ShapeDtypeStruct(keys.shape, bf16),
            jax.ShapeDtypeStruct(values.shape, bf16),
        ),
        in_specs=[pl.BlockSpec(memory_space=pl.ANY)] * 5 + [smem, smem],
        out_specs=(pl.BlockSpec(memory_space=pl.ANY), vmem, vmem),
        scratch_shapes=[
            pltpu.VMEM(out_grad.shape, bf16),
            pltpu.VMEM(queries.shape, bf16),
            pltpu.VMEM((nhead * chunks, features, chunk), bf16),
            pltpu.VMEM((far, chunks, count, chunk), bf16),
            pltpu.VMEM((count, features), f32),
            pltpu.VMEM((kv_local, columns, HEAD_DIM), bf16),
            pltpu.VMEM((kv_local, columns, HEAD_DIM), bf16),
            pltpu.VMEM((chips, 2, count, kv_local * HEAD_DIM), bf16),
            pltpu.VMEM((chips, 2, count, kv_local * HEAD_DIM), bf16),
            pltpu.VMEM((kv_local, chips, 2 * count, columns), f32),
            pltpu.VMEM((kv_local, chips, 1, columns), f32),
            pltpu.VMEM((kv_local, 1, columns), f32),
            pltpu.VMEM((kv_local, 1, columns), f32),
            pltpu.VMEM((2, chips, 2 * count, columns), f32),
            pltpu.VMEM((2, HEAD_DIM, columns), f32),
            pltpu.VMEM((kv_local, chips, 2, 2, count, HEAD_DIM), bf16),
            pltpu.VMEM((kv_local, chips, 2, count, HEAD_DIM), bf16),
            pltpu.VMEM((kv_local, 2, count, HEAD_DIM), f32),
            pltpu.VMEM((kv_local, chips, 2, count, HEAD_DIM), bf16),
            pltpu.VMEM((kv_local, chips, 2, count, HEAD_DIM), bf16),
            dma(()),
            dma((kv_local, GROUP)),
            dma((kv_local,)),
            dma((nhead * chunks,)),
            dma((far, chunks)),
            dma((far, chunks)),
            dma((chips,)),
            dma((chips,)),
            dma((chips, 2)),
            dma((chips, 2)),
            dma((chips,)),
            dma((chips,)),
            dma((kv_local, chips)),
            dma((kv_local, chips)),
            dma((kv_local, chips)),
            dma((kv_local, chips)),
        ],
        compiler_params=pltpu.CompilerParams(
            collective_id=0, has_side_effects=True, vmem_limit_bytes=60 * 1024 * 1024
        ),
    )(queries, keys, values, out_grad, out_weight, seq_lengths, prompt_lengths)
    anywhere = pl.BlockSpec(memory_space=pl.ANY)
    return pl.pallas_call(
        hand_on,
        out_shape=tuple(jax.ShapeDtypeStruct(r.shape, r.dtype) for r in results),
        in_specs=[anywhere] * 3,
        out_specs=(anywhere,) * 3,
        scratch_shapes=[pltpu.VMEM(r.shape, r.dtype) for r in results] + [dma((6,))],
        compiler_params=pltpu.CompilerParams(vmem_limit_bytes=60 * 1024 * 1024),
    )(*results)


def solution(mesh):
    return jax.shard_map(
        shards,
        mesh=mesh,
        in_specs=(
            P("ctx", "head"),
            P("ctx", "head"),
            P("ctx", "head"),
            P("ctx", "head"),
            P("head", None),
            P(),
            P(),
        ),
        out_specs=(P("ctx", "head"), P("ctx", "head"), P("ctx", "head")),
        check_vma=False,
    )
```
